128 devices in a mesh: dp: 8 (over x, y_lo), fsdp: 16 (over z, y_hi, core).
Axes of the slice: x: 4, y: 4 (y_hi: 2, y_lo: 2; y = y_hi * 2 + y_lo), z: 4, core: 2. Of those that a mesh axis runs over, the one named last changes fastest.
Arguments:
- activations: bfloat16 [16384, 8192], P(('dp', 'fsdp')), may hold values from -6 to 6
- out_grads: bfloat16 [16384, 28672], P(('dp', 'fsdp')), may hold values from -6 to 6
- act_signs: int32 [8192], replicated, may hold values 0 or 1
- grad_signs: int32 [28672], replicated, may hold values 0 or 1
- act_picks: int32 [2048], replicated, may hold values from 0 to 8191
- grad_picks: int32 [2048], replicated, may hold values from 0 to 28671
- gradient: bfloat16 [8192, 28672], P('dp', 'fsdp'), may hold values from -1100 to 1100, as said below
- damped_act: float32 [8192], P('dp'), may hold values from 0.25 to 2
- damped_grad: float32 [28672], P('fsdp'), may hold values from 0.25 to 2
- panel_act: bfloat16 [8192, 128], P(('dp', 'fsdp')), may hold values from -0.3125 to 0.3125
- panel_grad: bfloat16 [28672, 128], P(('fsdp', 'dp')), may hold values from -0.25 to 0.25
- core_act: float32 [128, 128], replicated, may hold values from -1 to 1, as said below
- core_grad: float32 [128, 128], replicated, may hold values from -1 to 1, as said below
Outputs:
- factor_act: float32 [8192, 2048], P(('fsdp', 'dp'))
- factor_grad: float32 [28672, 2048], P(('fsdp', 'dp'))
- update: float32 [8192, 28672], P('dp', 'fsdp')
The draws below stay inside these ranges and needn't reach their ends.
Inputs may be any that keep to these rules, and one draw needn't show every extreme that they name: `gradient`: A real matrix. `core_act`: Symmetric. `core_grad`: Symmetric.
All inputs are finite; a program needn't handle non-finite values.
Results may differ from the reference program's by a relative error of at most 0.02.
Values may be sent and summed in bfloat16 or wider, within the bound.
No kernel may reach another device: no remote copies, remote signals or barrier semaphores. Data moves between devices by JAX's collectives and lax.ppermute only.
A program may use at most 128 MiB of HBM per device.

```python
import math
import jax
import jax.numpy as jnp
from jax import lax

D = 8192
FF = 28672
K = 2048
RANK = 128
HB = 4096
TOK_DEV = 128
TOKENS = 16384
N_DP = 8
N_FSDP = 16


def assemble_core(diagonal, spread):
    size_rank = diagonal.shape[0]
    eye_mask = jnp.eye(size_rank, dtype=jnp.float32)
    symmetric = 0.5 * (spread + spread.T) * (0.4 * size_rank ** (-0.5))
    return symmetric * (1.0 - eye_mask) + eye_mask * diagonal[None, :]


def draw_gradient(key, part):
    key = jax.random.fold_in(key, 11)
    key_base, key_rows, key_cols = jax.random.split(key, 3)
    row_pos = jnp.arange(D, dtype=jnp.float32) / D
    col_pos = jnp.arange(FF, dtype=jnp.float32) / FF
    entries = jnp.clip(jax.random.normal(key_base, (D, FF), jnp.float32), -5.0, 5.0)
    ramp_power = 0.5
    row_scale = 3.0 ** (ramp_power * row_pos) * jnp.exp(jax.random.uniform(key_rows, (D,), jnp.float32, 0.0, 1.79))
    col_scale = 3.0 ** (ramp_power * col_pos) * jnp.exp(jax.random.uniform(key_cols, (FF,), jnp.float32, 0.0, 1.79))
    return (entries * row_scale[:, None] * col_scale[None, :]).astype(jnp.bfloat16)


def draw_core_act(key, part):
    key = jax.random.fold_in(key, 23)
    key_diag, key_off = jax.random.split(key, 2)
    diagonal = jax.random.uniform(key_diag, (RANK,), jnp.float32, 0.5, 1.0)
    spread = jnp.clip(jax.random.normal(key_off, (RANK, RANK), jnp.float32), -4.0, 4.0)
    return assemble_core(diagonal, spread)


def draw_core_grad(key, part):
    key = jax.random.fold_in(key, 37)
    key_diag, key_off = jax.random.split(key, 2)
    diagonal = jax.random.uniform(key_diag, (RANK,), jnp.float32, 0.5, 1.0)
    spread = jnp.clip(jax.random.normal(key_off, (RANK, RANK), jnp.float32), -4.0, 4.0)
    return assemble_core(diagonal, spread)


def set_ends(values, stream_key, smallest, high):
    longest = values.shape.index(max(values.shape))
    spots = []
    for shift in (0, 1):
        where = [jax.random.randint(jax.random.fold_in(stream_key, axis), (), 0, length) for axis, length in enumerate(values.shape)]
        where[longest] = (where[longest] + shift) % values.shape[longest]
        spots.append(tuple(where))
    return values.at[spots[0]].set(smallest).at[spots[1]].set(high)


def shard_levels(rng, dims, shards, least, high):
    factor_of = 1.0
    for dim, blocks in shards:
        draws = jax.random.uniform(jax.random.fold_in(jax.random.fold_in(rng, 6), dim), (blocks,), jnp.float32, least / len(shards), high / len(shards))
        factor_of = factor_of * jnp.repeat(jnp.exp(draws), dims[dim] // blocks).reshape((-1,) + (1,) * (len(dims) - 1 - dim))
    return factor_of


def noise(own_key, extent, scale, limit, cuts=(), held_as=jnp.bfloat16):
    loudness = shard_levels(own_key, extent, cuts, -0.22, 0.18) if cuts else 1.0
    result = jax.random.normal(own_key, extent, jnp.float32) * scale * loudness
    return jnp.minimum(jnp.maximum(result, -limit), limit).astype(held_as)


def setup_inputs(seed: int = 0) -> dict:
    seeds = jax.random.split(jax.random.key(seed), 14)
    return {
        "activations": noise(seeds[0], (TOKENS, D), 1.0, 6.0, ((0, 128),)),
        "out_grads": noise(seeds[1], (TOKENS, FF), 1.0, 6.0, ((0, 128),)),
        "act_signs": set_ends((jax.random.randint(seeds[2], (D,), 0, 2) < 1).astype(jnp.int32), jax.random.fold_in(seeds[2], 1), 0, 1),
        "grad_signs": set_ends((jax.random.randint(seeds[3], (FF,), 0, 2) < 1).astype(jnp.int32), jax.random.fold_in(seeds[3], 1), 0, 1),
        "act_picks": set_ends(jax.random.randint(seeds[4], (K,), 0, D), jax.random.fold_in(seeds[4], 1), 0, D - 1).astype(jnp.int32),
        "grad_picks": set_ends(jax.random.randint(seeds[5], (K,), 0, FF), jax.random.fold_in(seeds[5], 1), 0, FF - 1).astype(jnp.int32),
        "gradient": draw_gradient(jax.random.fold_in(seeds[13], 71), 0),
        "damped_act": jnp.clip(jnp.exp(math.log(2.0) - 2.0794415 * jax.random.uniform(seeds[7], (D,), jnp.float32) ** shard_levels(seeds[7], (D,), ((0, 8),), -0.2, 0.2)), 0.25, 2.0),
        "damped_grad": jnp.clip(jnp.exp(math.log(2.0) - 2.0794415 * jax.random.uniform(seeds[8], (FF,), jnp.float32) ** shard_levels(seeds[8], (FF,), ((0, 16),), -0.2, 0.2)), 0.25, 2.0),
        "panel_act": noise(seeds[9], (D, RANK), (0.7 * (D * RANK) ** -0.25), 0.3125, ((0, 128),)),
        "panel_grad": noise(seeds[10], (FF, RANK), (0.7 * (FF * RANK) ** -0.25), 0.25, ((0, 128),)),
        "core_act": draw_core_act(jax.random.fold_in(seeds[13], 71), 0),
        "core_grad": draw_core_grad(jax.random.fold_in(seeds[13], 71), 0),
    }


epsilon = 1e-06
clip_rms = 1.0

def hadamard_table(length):
    index = jnp.arange(length, dtype=jnp.int32)
    common = jnp.bitwise_and(index[:, None], index[None, :])
    parity = jnp.zeros((length, length), jnp.int32)
    for level in range(length.bit_length() - 1):
        parity = parity + jnp.bitwise_and(jnp.right_shift(common, level), 1)
    return (1 - 2 * (parity % 2)).astype(jnp.float32)

def hadamard_sketch(matrix, sign_bits, picked):
    row_count, col_count = matrix.shape
    inner_size = min(128, HB)
    outer_size = HB // inner_size
    sign_flip = (2 * sign_bits - 1).astype(jnp.bfloat16)
    signed = (matrix * sign_flip[None, :]).astype(jnp.float32)
    signed = signed.reshape(row_count, col_count // HB, outer_size, inner_size)
    inner_table = hadamard_table(inner_size).astype(jnp.float32)
    outer_table = hadamard_table(outer_size).astype(jnp.float32)
    section_one = jnp.einsum('tbqi,ij->tbqj', signed, inner_table, precision=lax.Precision.HIGHEST)
    section_two = jnp.einsum('tbqj,pq->tbpj', section_one, outer_table, precision=lax.Precision.HIGHEST)
    return jnp.take(section_two.reshape(row_count, col_count), picked, axis=1).astype(jnp.bfloat16)

def reference(activations, out_grads, act_signs, grad_signs, act_picks, grad_picks, gradient, damped_act, damped_grad, panel_act, panel_grad, core_act, core_grad):
    group_tokens = N_FSDP * TOK_DEV
    token_scale = 1.0 / TOKENS
    act_groups = activations.reshape(N_DP, group_tokens, D)
    grad_groups = out_grads.reshape(N_DP, group_tokens, FF)

    def group_step(carry, groups):
        act_rows, grad_rows = groups
        sketch_act = hadamard_sketch(act_rows, act_signs, act_picks)
        sketch_grad = hadamard_sketch(grad_rows, grad_signs, grad_picks)
        part_act = jnp.dot(act_rows.T, sketch_act, preferred_element_type=jnp.float32) * token_scale
        part_grad = jnp.dot(grad_rows.T, sketch_grad, preferred_element_type=jnp.float32) * token_scale
        part_act = part_act.astype(jnp.bfloat16).astype(jnp.float32)
        part_grad = part_grad.astype(jnp.bfloat16).astype(jnp.float32)
        return ((carry[0] + part_act, carry[1] + part_grad), None)
    start_carry = (jnp.zeros((D, K), jnp.float32), jnp.zeros((FF, K), jnp.float32))
    factors, unused = lax.scan(group_step, start_carry, (act_groups, grad_groups))
    factor_act, factor_grad = factors
    inv_act = 1.0 / damped_act
    inv_grad = 1.0 / damped_grad
    scaled_act = (panel_act * inv_act[:, None]).astype(jnp.bfloat16)
    scaled_grad = (panel_grad * inv_grad[:, None]).astype(jnp.bfloat16)
    left_sum = jnp.dot(scaled_act.T, gradient, preferred_element_type=jnp.float32)
    left_core = jnp.dot(core_act, left_sum, precision=lax.Precision.HIGHEST)
    left = inv_act[:, None] * gradient - jnp.dot(scaled_act.astype(jnp.float32), left_core, precision=lax.Precision.HIGHEST)
    left = left.astype(jnp.bfloat16)
    right_sum = jnp.dot(left, scaled_grad, preferred_element_type=jnp.float32)
    right_core = jnp.dot(right_sum, core_grad, precision=lax.Precision.HIGHEST)
    precon = left * inv_grad[None, :] - jnp.dot(right_core, scaled_grad.astype(jnp.float32).T, precision=lax.Precision.HIGHEST)
    total = jnp.sum(precon * precon)
    root_mean = jnp.sqrt(total / (D * FF) + epsilon)
    factor_clip = jnp.minimum(1.0, clip_rms / root_mean)
    return (factor_act, factor_grad, factor_clip * precon)
```

```python
import functools
import jax
import jax.numpy as jnp
from jax import lax
from jax.experimental import pallas as pl
from jax.experimental.pallas import tpu as pltpu
from jax.sharding import Mesh
from jax.sharding import PartitionSpec as P

BF = jnp.bfloat16
F32 = jnp.float32
HB = 4096
INNER = 256
OUTER = HB // INNER
MIB = 1 << 20


def hadamard_table(length):
    index = jnp.arange(length, dtype=jnp.int32)
    common = jnp.bitwise_and(index[:, None], index[None, :])
    parity = jnp.zeros((length, length), jnp.int32)
    for level in range(length.bit_length() - 1):
        parity = parity + jnp.bitwise_and(jnp.right_shift(common, level), 1)
    return (1 - 2 * (parity % 2)).astype(BF)


def sketch_kernel(picks, x_ref, sign_ref, table_ref, out_ref, inner, spread, rows):
    block = pl.program_id(0)
    for q in range(OUTER):
        cols = slice(q * INNER, (q + 1) * INNER)
        signed = table_ref[...] * sign_ref[:, cols]
        inner[q] = lax.dot_general(
            signed, x_ref[:, cols], (((1,), (1,)), ((), ())), preferred_element_type=F32
        )

    strip = 8

    def mix(j, carry):
        at = pl.ds(pl.multiple_of(j * strip, strip), strip)
        parts = [inner[q, at, :] for q in range(OUTER)]
        half = 1
        while half < OUTER:
            for low in range(OUTER):
                if low & half == 0:
                    a, b = parts[low], parts[low | half]
                    parts[low], parts[low | half] = a + b, a - b
            half *= 2
        for p in range(OUTER):
            to = pl.multiple_of(block * HB + p * INNER + j * strip, strip)
            spread[pl.ds(to, strip), :] = parts[p]
        return carry

    lax.fori_loop(0, INNER // strip, mix, 0, unroll=2)

    @pl.when(block == pl.num_programs(0) - 1)
    def _():
        count = rows.shape[0]
        group = 16

        def take(i, carry):
            base = pl.multiple_of(i * group, group)
            for k in range(group):
                rows[pl.ds(base + k, 1), :] = spread[pl.ds(picks[base + k], 1), :]
            return carry

        lax.fori_loop(0, count // group, take, 0)
        out_ref[...] = rows[...].T.astype(BF)


def sketch(matrix, signs, picks, table):
    tokens, width = matrix.shape
    count = picks.shape[0]
    sign_row = (2 * signs - 1).astype(BF)[None, :]
    return pl.pallas_call(
        sketch_kernel,
        grid_spec=pltpu.PrefetchScalarGridSpec(
            num_scalar_prefetch=1,
            grid=(width // HB,),
            in_specs=[
                pl.BlockSpec((tokens, HB), lambda b, p: (0, b)),
                pl.BlockSpec((1, HB), lambda b, p: (0, b)),
                pl.BlockSpec((INNER, INNER), lambda b, p: (0, 0)),
            ],
            out_specs=pl.BlockSpec((tokens, count), lambda b, p: (0, 0)),
            scratch_shapes=[
                pltpu.VMEM((OUTER, INNER, tokens), F32),
                pltpu.VMEM((width, tokens), F32),
                pltpu.VMEM((count, tokens), F32),
            ],
        ),
        out_shape=jax.ShapeDtypeStruct((tokens, count), BF),
        compiler_params=pltpu.CompilerParams(vmem_limit_bytes=32 * MIB),
        cost_estimate=pl.CostEstimate(
            flops=4 * tokens * width * INNER, bytes_accessed=2 * tokens * (width + count), transcendentals=0
        ),
        name="sketch",
    )(picks, matrix, sign_row, table)


def pick_kernel(coords, grad_ref, act_ref, out_ref):
    wide = grad_ref.shape[1]
    out_ref[:, :wide] = grad_ref[...]
    out_ref[:, wide:] = act_ref[...]


def pick_sibling(coords, grads, acts, slabs):
    tokens = grads.shape[0]
    wide, slim = grads.shape[1] // (2 * slabs), acts.shape[1] // (2 * slabs)
    return pl.pallas_call(
        pick_kernel,
        grid_spec=pltpu.PrefetchScalarGridSpec(
            num_scalar_prefetch=1,
            grid=(slabs,),
            in_specs=[
                pl.BlockSpec((tokens, wide), lambda i, c: (0, 2 * i + 1 - c[3])),
                pl.BlockSpec((tokens, slim), lambda i, c: (0, 2 * i + 1 - c[3])),
            ],
            out_specs=pl.BlockSpec((tokens, wide + slim), lambda i, c: (0, i)),
        ),
        out_shape=jax.ShapeDtypeStruct((tokens, slabs * (wide + slim)), BF),
        cost_estimate=pl.CostEstimate(
            flops=0, bytes_accessed=4 * tokens * slabs * (wide + slim), transcendentals=0
        ),
        name="pick_sibling",
    )(coords, grads, acts)


def turn_kernel(coords, grad_ref, act_ref, sib_ref, *refs):
    outs_z, outs_x, outs_y = refs[0:4], refs[4:8], refs[8:12]
    turned_grad, turned_act = refs[12:]
    dz, yhi = pl.program_id(0), pl.program_id(1)
    x, y = coords[0], coords[1]
    wide = grad_ref.shape[1]
    own = wide // 8
    part = own // 2
    small = act_ref.shape[1] // 8
    turned_grad[...] = jnp.concatenate([grad_ref[...], sib_ref[:, :wide]], axis=0).T
    turned_act[...] = jnp.concatenate([act_ref[...], sib_ref[:, wide:]], axis=0).T
    for dx in range(4):
        xp = (x + dx) & 3
        for ylo in range(2):
            dy = (2 * yhi + ylo - y) & 3
            at = pl.multiple_of(xp * (2 * own) + ylo * own, 16)
            outs_x[dx][dy * 4 + dz] = turned_grad[pl.ds(at + part, part), :]
    for j in range(4):

        @pl.when(dz == j)
        def _(j=j):
            for dx in range(4):
                xp = (x + dx) & 3
                for ylo in range(2):
                    dy = (2 * yhi + ylo - y) & 3
                    at = pl.multiple_of(xp * (2 * own) + ylo * own, 16)
                    outs_z[j][dx * 4 + dy] = turned_grad[pl.ds(at, part), :]

    for dy in range(4):
        yp = (y + dy) & 3

        @pl.when((yp >> 1) == yhi)
        def _(dy=dy, yp=yp):
            for dx in range(4):
                at = pl.multiple_of(((x + dx) & 3) * (2 * small) + (yp & 1) * small, 16)
                outs_y[dy][dz * 4 + dx] = turned_act[pl.ds(at, small), :]


def turn(coords, grads, acts, sibling):
    tokens = grads.shape[0]
    wide, slim = grads.shape[1] // 16, acts.shape[1] // 16
    part, small = wide // 16, slim // 8

    def slab(i, j, c):
        return (0, ((c[2] + i) & 3) * 4 + j * 2 + c[3])

    def pair(i, j, c):
        return (0, ((c[2] + i) & 3) * 2 + j)

    shape_grad = jax.ShapeDtypeStruct((16, part, 2 * tokens), BF)
    shape_act = jax.ShapeDtypeStruct((16, small, 2 * tokens), BF)
    whole = lambda i, j, c: (0, 0, 0)
    outs = pl.pallas_call(
        turn_kernel,
        grid_spec=pltpu.PrefetchScalarGridSpec(
            num_scalar_prefetch=1,
            grid=(4, 2),
            in_specs=[
                pl.BlockSpec((tokens, wide), slab),
                pl.BlockSpec((tokens, slim), slab),
                pl.BlockSpec((tokens, wide + slim), pair),
            ],
            out_specs=[pl.BlockSpec((16, part, 2 * tokens), whole)] * 8
            + [pl.BlockSpec((16, small, 2 * tokens), whole)] * 4,
            scratch_shapes=[
                pltpu.VMEM((wide, 2 * tokens), BF),
                pltpu.VMEM((slim, 2 * tokens), BF),
            ],
        ),
        out_shape=[shape_grad] * 8 + [shape_act] * 4,
        compiler_params=pltpu.CompilerParams(vmem_limit_bytes=40 * MIB),
        cost_estimate=pl.CostEstimate(
            flops=0, bytes_accessed=8 * tokens * 8 * (wide + slim), transcendentals=0
        ),
        name="turn",
    )(coords, grads, acts, sibling)
    flat = [o.reshape(-1, 2 * tokens) for o in outs]
    return flat[0:4], flat[4:8], flat[8:12]


def part_kernel(scale, n_out, *refs):
    rows, own, sib = refs[0:4], refs[4:8], refs[8]
    outs = refs[9:]
    tokens = own[0].shape[0]
    total = None
    for d in range(4):
        keys = jnp.concatenate([own[d][...], sib[d * tokens : (d + 1) * tokens, :]], axis=0)
        term = jnp.dot(rows[d][...], keys, preferred_element_type=F32)
        total = term if total is None else total + term
    total = (total * scale).astype(BF)
    if n_out == 1:
        outs[0][...] = total
    else:
        for j in range(n_out):

            @pl.when(pl.program_id(0) * n_out // pl.num_programs(0) == j)
            def _(j=j):
                outs[j][...] = total


def part_product(rows, own, sib, scale, first, count, n_out, tile):
    tokens, width = own[0].shape
    each = count // n_out
    steps = count // tile
    per = each // tile
    in_specs = (
        [pl.BlockSpec((tile, 2 * tokens), lambda i: (i + first // tile, 0))] * 4
        + [pl.BlockSpec((tokens, width), lambda i: (0, 0))] * 4
        + [pl.BlockSpec((4 * tokens, width), lambda i: (0, 0))]
    )

    def place(j):
        return lambda i: (jnp.clip(i - j * per, 0, per - 1), 0)

    return pl.pallas_call(
        functools.partial(part_kernel, scale, n_out),
        grid=(steps,),
        in_specs=in_specs,
        out_specs=[pl.BlockSpec((tile, width), place(j)) for j in range(n_out)],
        out_shape=[jax.ShapeDtypeStruct((each, width), BF)] * n_out,
        compiler_params=pltpu.CompilerParams(vmem_limit_bytes=40 * MIB),
        cost_estimate=pl.CostEstimate(
            flops=2 * count * 8 * tokens * width,
            bytes_accessed=2 * (count * 8 * tokens + 8 * tokens * width + count * width),
            transcendentals=0,
        ),
        name="part_product",
    )(*rows, *own, sib)


AXES = ("x", "ylo", "z", "yhi", "core")
GROUP = ("z", "yhi", "core")
DATA = ("x", "ylo")
RING_Y = ("ylo", "yhi")
epsilon = 1e-06
clip_rms = 1.0


def shift(array, axis, step):
    if axis == "y":
        spot = lambda y: (y % 2) * 2 + y // 2
        return lax.ppermute(
            array, RING_Y, [(spot(y), spot((y + step) % 4)) for y in range(4)]
        )
    return lax.ppermute(array, axis, [(i, (i + step) % 4) for i in range(4)])


def swap(array):
    return lax.ppermute(array, "core", [(0, 1), (1, 0)])


def spread_sketch(own, axis):
    got = [own] + [shift(own, axis, d) for d in (1, 2, 3)]
    return got, swap(jnp.concatenate(got, axis=0))


def add(first, second):
    return first.astype(F32) + second.astype(F32)


def reduce_part(rows, keys, axes, scale):
    own, sib = keys
    quarter = rows[0].shape[0] // 4
    half = quarter // 2
    first, second = axes
    far = part_product(rows, own, sib, scale, 2 * quarter, quarter, 2, half)
    via = [shift(far[0], first, 1), shift(far[1], first, 3)]
    (one,) = part_product(rows, own, sib, scale, quarter, quarter, 1, half)
    (three,) = part_product(rows, own, sib, scale, 3 * quarter, quarter, 1, half)
    one = jnp.concatenate([add(one[:half], via[0]).astype(BF), one[half:]], axis=0)
    three = jnp.concatenate([three[:half], add(three[half:], via[1]).astype(BF)], axis=0)
    near = [shift(one, first, 1), shift(three, first, 3)]
    (here,) = part_product(rows, own, sib, scale, 0, quarter, 1, half)
    total = add(here, near[0]) + near[1].astype(F32)
    block = quarter // 4
    sent = [total[d * block : (d + 1) * block].astype(BF) for d in (1, 2, 3)]
    got = [shift(s, second, d) for d, s in zip((1, 2, 3), sent)]
    return total[:block] + got[0].astype(F32) + got[1].astype(F32) + got[2].astype(F32)


def contract_rows(first_block, second_block):
    return lax.dot_general(
        first_block, second_block, (((0,), (0,)), ((), ())), preferred_element_type=F32
    )


def split_parts(matrix):
    high_part = matrix.astype(BF)
    low_part = (matrix - high_part.astype(F32)).astype(BF)
    return high_part, low_part


def expand_rows(panel, core_product):
    high_part, low_part = split_parts(core_product)
    return jnp.dot(panel, high_part, preferred_element_type=F32) + jnp.dot(
        panel, low_part, preferred_element_type=F32
    )


def expand_cols(core_product, panel):
    high_part, low_part = split_parts(core_product)
    dims = (((1,), (1,)), ((), ()))
    return lax.dot_general(
        high_part, panel, dims, preferred_element_type=F32
    ) + lax.dot_general(low_part, panel, dims, preferred_element_type=F32)


def share(block, axes, n):
    copies = jnp.broadcast_to(block[None], (n,) + block.shape)
    return lax.all_to_all(copies, axes, 0, 0, tiled=True)


def deal(blocks, axes):
    return lax.all_to_all(blocks, axes, 0, 0, tiled=True).astype(F32).sum(0)


def precondition(gradient, damped_act, damped_grad, panel_act, panel_grad, core_act, core_grad):
    n_data, n_group = lax.axis_size(DATA), lax.axis_size(GROUP)
    rows, cols = gradient.shape
    rank = panel_act.shape[1]
    inv_act = 1.0 / damped_act
    inv_grad = 1.0 / damped_grad
    rows_act = share(panel_act, GROUP, n_group).reshape(rows, rank)
    rows_grad = share(panel_grad, DATA, n_data).reshape(cols, rank)
    scaled_act = (rows_act * inv_act[:, None]).astype(BF)
    scaled_grad = (rows_grad * inv_grad[:, None]).astype(BF)
    left_part = contract_rows(scaled_act, gradient).astype(BF)
    left_sum = deal(left_part.reshape(n_data, rank // n_data, cols), DATA).astype(BF)
    left_sum = share(left_sum, DATA, n_data).reshape(rank, cols).astype(F32)
    left_core = jnp.dot(core_act, left_sum, precision=lax.Precision.HIGHEST)
    left = inv_act[:, None] * gradient - expand_rows(scaled_act, left_core)
    left = left.astype(BF)
    right_part = jnp.dot(left, scaled_grad, preferred_element_type=F32).astype(BF)
    right_sum = deal(right_part.reshape(n_group, rows // n_group, rank), GROUP).astype(BF)
    right_sum = share(right_sum, GROUP, n_group).reshape(rows, rank).astype(F32)
    right_core = jnp.dot(right_sum, core_grad, precision=lax.Precision.HIGHEST)
    precon = left * inv_grad[None, :] - expand_cols(right_core, scaled_grad)
    total = jnp.sum(precon * precon)
    total = share(jnp.full((8, 128), total, F32), GROUP, n_group).sum(0)
    total = share(total, DATA, n_data).sum(0)[0, 0]
    entries_all = rows * n_data * cols * n_group
    root_mean = jnp.sqrt(total / entries_all + epsilon)
    return jnp.minimum(1.0, clip_rms / root_mean) * precon


def local(
    activations,
    out_grads,
    act_signs,
    grad_signs,
    act_picks,
    grad_picks,
    gradient,
    damped_act,
    damped_grad,
    panel_act,
    panel_grad,
    core_act,
    core_grad,
):
    y = lax.axis_index("yhi") * 2 + lax.axis_index("ylo")
    coords = jnp.stack(
        [lax.axis_index("x"), y, lax.axis_index("z"), lax.axis_index("core")]
    ).astype(jnp.int32)
    token_scale = 1.0 / (activations.shape[0] * lax.axis_size(AXES))
    table = hadamard_table(INNER)
    sibling = swap(pick_sibling(coords, out_grads, activations, 8))
    sketch_grad = sketch(out_grads, grad_signs, grad_picks, table)
    sketch_act = sketch(activations, act_signs, act_picks, table)
    for_z, for_x, for_y = turn(coords, out_grads, activations, sibling)
    rows_z = for_z[:1] + [shift(for_z[d], "z", d) for d in (1, 2, 3)]
    rows_x = for_x[:1] + [shift(for_x[d], "x", d) for d in (1, 2, 3)]
    rows_y = for_y[:1] + [shift(for_y[d], "y", d) for d in (1, 2, 3)]
    keys_z = spread_sketch(sketch_grad, "z")
    keys_x = spread_sketch(sketch_grad, "x")
    keys_y = spread_sketch(sketch_act, "y")
    done_z = reduce_part(rows_z, keys_z, ("x", "y"), token_scale)
    done_x = reduce_part(rows_x, keys_x, ("y", "z"), token_scale)
    factor_act = reduce_part(rows_y, keys_y, ("z", "x"), token_scale)
    factor_grad = jnp.concatenate([done_z, done_x], axis=0)
    update = precondition(
        gradient, damped_act, damped_grad, panel_act, panel_grad, core_act, core_grad
    )
    return factor_act, factor_grad, update


def solution(mesh):
    cut = Mesh(mesh.devices.reshape(4, 2, 4, 2, 2), AXES)
    placed = (
        P(AXES, None),
        P(AXES, None),
        P(),
        P(),
        P(),
        P(),
        P(DATA, GROUP),
        P(DATA),
        P(GROUP),
        P(AXES, None),
        P(GROUP + DATA, None),
        P(),
        P(),
    )
    return jax.shard_map(
        local,
        mesh=cut,
        in_specs=placed,
        out_specs=(P(GROUP + DATA, None), P(GROUP + DATA, None), P(DATA, GROUP)),
        check_vma=False,
    )
```

```python
import functools
import jax
import jax.numpy as jnp
import numpy as np
from jax import lax
from jax.experimental import pallas as pl
from jax.experimental.pallas import tpu as pltpu
from jax.sharding import Mesh
from jax.sharding import PartitionSpec as P

BF = jnp.bfloat16
F32 = jnp.float32
HB = 4096
INNER = 256
OUTER = HB // INNER
ROOM = 60 << 20


def hadamard_table(length):
    table = np.ones((1, 1), np.float32)
    while table.shape[0] < length:
        table = np.block([[table, table], [table, -table]])
    return jnp.asarray(table, BF)


def sketch_kernel(picks, x_ref, sign_ref, table_ref, out_ref, inner, spread, rows):
    block = pl.program_id(0)
    signs = (2 * sign_ref[...] - 1).astype(F32).astype(BF)
    for q in range(OUTER):
        cols = slice(q * INNER, (q + 1) * INNER)
        signed = table_ref[...] * signs[:, cols]
        inner[q] = lax.dot_general(
            signed, x_ref[:, cols], (((1,), (1,)), ((), ())), preferred_element_type=F32
        )

    strip = 8

    def mix(j, carry):
        at = pl.ds(pl.multiple_of(j * strip, strip), strip)
        parts = [inner[q, at, :] for q in range(OUTER)]
        half = 1
        while half < OUTER:
            for low in range(OUTER):
                if low & half == 0:
                    a, b = parts[low], parts[low | half]
                    parts[low], parts[low | half] = a + b, a - b
            half *= 2
        for p in range(OUTER):
            to = pl.multiple_of(block * HB + p * INNER + j * strip, strip)
            spread[pl.ds(to, strip), :] = parts[p]
        return carry

    lax.fori_loop(0, INNER // strip, mix, 0, unroll=2)

    @pl.when(block == pl.num_programs(0) - 1)
    def _():
        count = rows.shape[0]
        group = 16

        def take(i, carry):
            base = pl.multiple_of(i * group, group)
            for k in range(group):
                rows[pl.ds(base + k, 1), :] = spread[pl.ds(picks[base + k], 1), :]
            return carry

        lax.fori_loop(0, count // group, take, 0)
        out_ref[...] = rows[...].T.astype(BF)


def sketch(matrix, signs, picks, table):
    tokens, width = matrix.shape
    count = picks.shape[0]
    return pl.pallas_call(
        sketch_kernel,
        grid_spec=pltpu.PrefetchScalarGridSpec(
            num_scalar_prefetch=1,
            grid=(width // HB,),
            in_specs=[
                pl.BlockSpec((tokens, HB), lambda b, p: (0, b)),
                pl.BlockSpec((1, HB), lambda b, p: (0, b)),
                pl.BlockSpec((INNER, INNER), lambda b, p: (0, 0)),
            ],
            out_specs=pl.BlockSpec((tokens, count), lambda b, p: (0, 0)),
            scratch_shapes=[
                pltpu.VMEM((OUTER, INNER, tokens), F32),
                pltpu.VMEM((width, tokens), F32),
                pltpu.VMEM((count, tokens), F32),
            ],
        ),
        out_shape=jax.ShapeDtypeStruct((tokens, count), BF),
        compiler_params=pltpu.CompilerParams(vmem_limit_bytes=ROOM),
        cost_estimate=pl.CostEstimate(
            flops=4 * tokens * width * INNER, bytes_accessed=2 * tokens * (width + count), transcendentals=0
        ),
        name="sketch",
    )(picks, matrix, signs[None, :], table)


def turn_kernel(shifts, coords, grad_ref, *refs):
    outs, turned = refs[:-1], refs[-1]
    yhi = pl.program_id(1)
    x, y, core = coords[0], coords[1], coords[3]
    wide = grad_ref.shape[1] // 2
    own = wide // 8
    part = own // 2
    turned[...] = grad_ref[...].T
    for j in range(len(shifts)):

        @pl.when(pl.program_id(0) == j)
        def _(j=j):
            for away in range(2):
                for dx in range(4):
                    for ylo in range(2):
                        dy = (2 * yhi + ylo - y) & 3
                        at = (core ^ away) * wide + ((x + dx) & 3) * (2 * own) + ylo * own
                        at = pl.multiple_of(at, 16)
                        out = outs[2 * j + away]
                        out[dx * 4 + dy] = turned[pl.ds(at, part), :]
                        out[16 + dy * 4 + dx] = turned[pl.ds(at + part, part), :]


def turn(coords, grads, shifts):
    tokens = grads.shape[0]
    wide = grads.shape[1] // 8
    part = wide // 32
    first, last = shifts[0], shifts[-1]

    def slab(i, j, c):
        return (0, ((c[2] + jnp.where(i == 0, first, last)) & 3) * 2 + j)

    count = 2 * len(shifts)
    outs = pl.pallas_call(
        functools.partial(turn_kernel, shifts),
        grid_spec=pltpu.PrefetchScalarGridSpec(
            num_scalar_prefetch=1,
            grid=(len(shifts), 2),
            in_specs=[pl.BlockSpec((tokens, wide), slab)],
            out_specs=[pl.BlockSpec((32, part, tokens), lambda i, j, c: (0, 0, 0))] * count,
            scratch_shapes=[pltpu.VMEM((wide, tokens), BF)],
        ),
        out_shape=[jax.ShapeDtypeStruct((32, part, tokens), BF)] * count,
        compiler_params=pltpu.CompilerParams(vmem_limit_bytes=ROOM),
        cost_estimate=pl.CostEstimate(
            flops=0, bytes_accessed=4 * tokens * 2 * len(shifts) * wide, transcendentals=0
        ),
        name="turn",
    )(coords, grads)
    return [o.reshape(-1, tokens) for o in outs]


def turn_act_kernel(act_ref, out_ref, turned):
    z, yhi = pl.program_id(0), pl.program_id(1)
    slim = act_ref.shape[1] // 2
    small = slim // 8
    turned[...] = act_ref[...].T
    for ylo in range(2):
        for side in range(2):
            for xp in range(4):
                at = side * slim + xp * (2 * small) + ylo * small
                out_ref[ylo * 4 + yhi * 2 + side, xp * 4 + z] = turned[at : at + small, :]


def turn_act(acts):
    tokens = acts.shape[0]
    slim = acts.shape[1] // 8
    small = slim // 16
    return pl.pallas_call(
        turn_act_kernel,
        grid=(4, 2),
        in_specs=[pl.BlockSpec((tokens, slim), lambda i, j: (0, i * 2 + j))],
        out_specs=pl.BlockSpec((8, 16, small, tokens), lambda i, j: (0, 0, 0, 0)),
        out_shape=jax.ShapeDtypeStruct((8, 16, small, tokens), BF),
        scratch_shapes=[pltpu.VMEM((slim, tokens), BF)],
        compiler_params=pltpu.CompilerParams(vmem_limit_bytes=ROOM),
        cost_estimate=pl.CostEstimate(
            flops=0, bytes_accessed=4 * tokens * 8 * slim, transcendentals=0
        ),
        name="turn_act",
    )(acts)


def part_kernel(scale, split, coords, *refs):
    rows, given, outs = refs[0:8], refs[8:16], refs[16:]
    total = None
    for d in range(0, 8, 2):
        block = jnp.concatenate([rows[d][...], rows[d + 1][...]], axis=1)
        keys = jnp.concatenate([given[d][...], given[d + 1][...]], axis=0)
        term = jnp.dot(block, keys, preferred_element_type=F32)
        total = term if total is None else total + term
    total = (total * scale).astype(BF)
    if split == 0:
        outs[0][...] = total
        return
    each = total.shape[0] // split
    for j in range(len(outs) // split):

        @pl.when(pl.program_id(0) == j)
        def _(j=j):
            for k in range(split):
                outs[j * split + k][...] = total[k * each : (k + 1) * each]


def part_product(coords, rows, row_specs, keys, key_specs, scale, tile, steps, split):
    tokens, width = rows[0].shape[-1], keys[0].shape[-1]
    if split:
        each, count = tile // split, steps * split
        out_spec = pl.BlockSpec((each, width), lambda i, c: (0, 0))
    else:
        each, count = tile * steps, 1
        out_spec = pl.BlockSpec((tile, width), lambda i, c: (i, 0))
    return pl.pallas_call(
        functools.partial(part_kernel, scale, split),
        grid_spec=pltpu.PrefetchScalarGridSpec(
            num_scalar_prefetch=1,
            grid=(steps,),
            in_specs=row_specs + key_specs,
            out_specs=[out_spec] * count,
        ),
        out_shape=[jax.ShapeDtypeStruct((each, width), BF)] * count,
        compiler_params=pltpu.CompilerParams(vmem_limit_bytes=ROOM),
        cost_estimate=pl.CostEstimate(
            flops=2 * steps * tile * 8 * tokens * width,
            bytes_accessed=2 * (steps * tile * (8 * tokens + width) + 8 * tokens * width),
            transcendentals=0,
        ),
        name="part_product",
    )(coords, *rows, *keys)


def part_grad(coords, rows, keys, scale, tiles, split=1):
    tile, tokens = rows[0].shape[0] // 8, rows[0].shape[1]
    width = keys.shape[-1]

    def at(i):
        place = tiles[0]
        for j in range(1, len(tiles)):
            place = jnp.where(i >= j, tiles[j], place)
        return place

    def member(d, c):
        return ((c[2] - d // 2) & 3) * 2 + (c[3] ^ (d % 2))

    row_spec = pl.BlockSpec((tile, tokens), lambda i, c: (at(i), 0))
    key_specs = [
        pl.BlockSpec((None, tokens, width), lambda i, c, d=d: (member(d, c), 0, 0))
        for d in range(8)
    ]
    return part_product(
        coords, rows, [row_spec] * 8, [keys] * 8, key_specs, scale, tile, len(tiles), split
    )


def part_act(coords, rows, keys, sibling, scale):
    tile, tokens = rows.shape[1] // 4, rows.shape[2]
    width = sibling.shape[-1]

    def member(d, away, c):
        y = (c[1] - d) & 3
        return (y & 1) * 4 + (y >> 1) * 2 + (c[3] ^ away)

    row_specs = [
        pl.BlockSpec((None, tile, tokens), lambda i, c, d=d, a=a: (member(d, a, c), i, 0))
        for a in range(2)
        for d in range(4)
    ]
    key_specs = [pl.BlockSpec((tokens, width), lambda i, c: (0, 0))] * 4
    key_specs += [pl.BlockSpec((tokens, width), lambda i, c, d=d: (d, 0)) for d in range(4)]
    return part_product(
        coords, [rows] * 8, row_specs, [*keys, *([sibling] * 4)], key_specs, scale, tile, 4, 0
    )[0]


def add_kernel(*refs):
    count = len(refs) // 3
    for j in range(count):
        base, term, out = refs[j], refs[count + j], refs[2 * count + j]
        out[...] = (base[...].astype(F32) + term[...].astype(F32)).astype(BF)


def add_terms(bases, terms):
    rows, width = terms[0].shape
    block = rows // 2
    count = len(bases)
    spec = pl.BlockSpec((block, width), lambda i: (i, 0))
    return pl.pallas_call(
        add_kernel,
        grid=(2,),
        in_specs=[spec] * (2 * count),
        out_specs=[spec] * count,
        out_shape=[jax.ShapeDtypeStruct(b.shape, BF) for b in bases],
        compiler_params=pltpu.CompilerParams(vmem_limit_bytes=ROOM),
        cost_estimate=pl.CostEstimate(
            flops=count * rows * width, bytes_accessed=6 * count * rows * width, transcendentals=0
        ),
        name="add_terms",
    )(*bases, *terms)


def merge_kernel(*refs):
    count = len(refs) // 9
    ins, outs = refs[: 5 * count], refs[5 * count :]
    for p in range(count):
        here, *halves = [r[...].astype(F32) for r in ins[5 * p : 5 * p + 5]]
        half = here.shape[0] // 2
        total = [here[:half] + halves[0] + halves[2], here[half:] + halves[1] + halves[3]]
        block = half // 2
        outs[4 * p][...] = total[0][:block]
        outs[4 * p + 1][...] = total[0][block:].astype(BF)
        outs[4 * p + 2][...] = total[1][:block].astype(BF)
        outs[4 * p + 3][...] = total[1][block:].astype(BF)


def merge(groups):
    rows, width = groups[0][0].shape
    block, cols = rows // 4, width // 4
    count = len(groups)
    outs = pl.pallas_call(
        merge_kernel,
        grid=(4,),
        in_specs=(
            [pl.BlockSpec((rows, cols), lambda i: (0, i))]
            + [pl.BlockSpec((rows // 2, cols), lambda i: (0, i))] * 4
        )
        * count,
        out_specs=[pl.BlockSpec((block, cols), lambda i: (0, i))] * (4 * count),
        out_shape=(
            [jax.ShapeDtypeStruct((block, width), F32)]
            + [jax.ShapeDtypeStruct((block, width), BF)] * 3
        )
        * count,
        compiler_params=pltpu.CompilerParams(vmem_limit_bytes=ROOM),
        cost_estimate=pl.CostEstimate(
            flops=2 * count * rows * width,
            bytes_accessed=9 * count * rows * width,
            transcendentals=0,
        ),
        name="merge",
    )(*[a for g in groups for a in g])
    return [outs[4 * p : 4 * p + 4] for p in range(count)]


def finish_kernel(*refs):
    out = refs[-1]
    block = refs[0].shape[0]
    for part in range(2):
        own, *got = refs[4 * part : 4 * part + 4]
        total = own[...]
        for g in got:
            total = total + g[...].astype(F32)
        out[part * block : (part + 1) * block] = total


def finish(first, second):
    rows, width = first[0].shape
    cols = width // 2
    return pl.pallas_call(
        finish_kernel,
        grid=(2,),
        in_specs=[pl.BlockSpec((rows, cols), lambda i: (0, i))] * 8,
        out_specs=pl.BlockSpec((2 * rows, cols), lambda i: (0, i)),
        out_shape=jax.ShapeDtypeStruct((2 * rows, width), F32),
        cost_estimate=pl.CostEstimate(
            flops=6 * rows * width, bytes_accessed=28 * rows * width, transcendentals=0
        ),
        compiler_params=pltpu.CompilerParams(vmem_limit_bytes=ROOM),
        name="finish",
    )(*first, *second)


AXES = ("x", "ylo", "z", "yhi", "core")
GROUP = ("z", "yhi", "core")
DATA = ("x", "ylo")
RING_Y = ("ylo", "yhi")
AROUND_Y = ("ylo", "yhi", "core")
ALONG_Z = ("z", "core")
epsilon = 1e-06
clip_rms = 1.0


def shift(array, axis, step):
    if axis == "y":
        spot = lambda y: (y % 2) * 2 + y // 2
        return lax.ppermute(
            array, RING_Y, [(spot(y), spot((y + step) % 4)) for y in range(4)]
        )
    return lax.ppermute(array, axis, [(i, (i + step) % 4) for i in range(4)])


def swap(array):
    return lax.ppermute(array, "core", [(0, 1), (1, 0)])


def send(array, step, away):
    pairs = [(2 * z + c, 2 * ((z + step) % 4) + (c ^ away)) for z in range(4) for c in range(2)]
    return lax.ppermute(array, ALONG_Z, pairs)


def phase(*values):
    return lax.optimization_barrier(values)


def contract_rows(first_block, second_block):
    return lax.dot_general(
        first_block, second_block, (((0,), (0,)), ((), ())), preferred_element_type=F32
    )


def split_parts(matrix):
    high_part = matrix.astype(BF)
    low_part = (matrix - high_part.astype(F32)).astype(BF)
    return high_part, low_part


def expand_rows(panel, core_product):
    high_part, low_part = split_parts(core_product)
    return jnp.dot(panel, high_part, preferred_element_type=F32) + jnp.dot(
        panel, low_part, preferred_element_type=F32
    )


def expand_cols(core_product, panel):
    high_part, low_part = split_parts(core_product)
    dims = (((1,), (1,)), ((), ()))
    return lax.dot_general(
        high_part, panel, dims, preferred_element_type=F32
    ) + lax.dot_general(low_part, panel, dims, preferred_element_type=F32)


def share(block, axes, n):
    copies = jnp.broadcast_to(block[None], (n,) + block.shape)
    return lax.all_to_all(copies, axes, 0, 0, tiled=True)


def deal(blocks, axes):
    return lax.all_to_all(blocks, axes, 0, 0, tiled=True).astype(F32).sum(0)


def local(
    activations,
    out_grads,
    act_signs,
    grad_signs,
    act_picks,
    grad_picks,
    gradient,
    damped_act,
    damped_grad,
    panel_act,
    panel_grad,
    core_act,
    core_grad,
):
    y = lax.axis_index("yhi") * 2 + lax.axis_index("ylo")
    coords = jnp.stack(
        [lax.axis_index("x"), y, lax.axis_index("z"), lax.axis_index("core")]
    ).astype(jnp.int32)
    token_scale = 1.0 / (activations.shape[0] * lax.axis_size(AXES))
    table = hadamard_table(INNER)
    n_data, n_group = lax.axis_size(DATA), lax.axis_size(GROUP)
    rows, cols = gradient.shape
    rank = panel_act.shape[1]
    inv_act = 1.0 / damped_act
    inv_grad = 1.0 / damped_grad

    rows_act = share(panel_act, GROUP, n_group).reshape(rows, rank)
    sketch_act = sketch(activations, act_signs, act_picks, table)
    for_y = turn_act(activations)
    here, here_away, two, two_away = turn(coords, out_grads, (0, 2))
    (rows_act, two, two_away, here_away, sketch_act, for_y, coords, gradient, grad_picks) = phase(
        rows_act, two, two_away, here_away, sketch_act, for_y, coords, gradient, grad_picks
    )

    got = [send(two, 2, 0), send(two_away, 2, 1)]
    keys_y = [sketch_act] + [shift(sketch_act, "y", d) for d in (1, 2, 3)]
    rows_y = lax.all_to_all(for_y, AROUND_Y, 0, 0, tiled=True).reshape(8, -1, for_y.shape[-1])
    one, one_away, three, three_away = turn(coords, out_grads, (1, 3))
    sketch_grad = sketch(out_grads, grad_signs, grad_picks, table)
    scaled_act = (rows_act * inv_act[:, None]).astype(BF)
    left_part = contract_rows(scaled_act, gradient).astype(BF)
    left_part = left_part.reshape(n_data, rank // n_data, cols)
    panel = jnp.broadcast_to(panel_grad.reshape(1, -1, cols), (n_data, rank // n_data, cols))
    mixed = jnp.concatenate([left_part, panel], axis=1)
    (got, one, one_away, three, three_away, rows_y, mixed, sketch_grad, keys_y, scaled_act) = phase(
        got, one, one_away, three, three_away, rows_y, mixed, sketch_grad, keys_y, scaled_act
    )
    got_two, got_two_away = got

    keys_z = lax.all_gather(sketch_grad, ALONG_Z, axis=0)
    got = [send(one, 1, 0), send(three, 3, 0), send(here_away, 0, 1)]
    both = jnp.concatenate(keys_y, axis=0)
    mixed = lax.all_to_all(mixed, DATA, 0, 0, tiled=True)
    (got, one_away, three_away, both, mixed) = phase(got, one_away, three_away, both, mixed)
    got_one, got_three, got_here_away = got
    left_sum = mixed[:, : rank // n_data].astype(F32).sum(0).astype(BF)
    keys_sib = swap(both)
    (left_sum, mixed, keys_sib, one_away, three_away) = phase(
        left_sum, mixed, keys_sib, one_away, three_away
    )

    got = [send(one_away, 1, 1), send(three_away, 3, 1)]
    left_sum = share(left_sum, DATA, n_data).reshape(rank, cols)
    rows_grad = mixed[:, rank // n_data :].reshape(cols, rank)
    scaled_grad = (rows_grad * inv_grad[:, None]).astype(BF)
    partial = part_act(coords, rows_y, keys_y, keys_sib, token_scale)
    (got, left_sum, scaled_grad, partial, keys_z) = phase(got, left_sum, scaled_grad, partial, keys_z)
    got_one_away, got_three_away = got
    factor_act = lax.psum_scatter(partial, ("x", "z"), scatter_dimension=0, tiled=True).astype(F32)

    left_core = jnp.dot(core_act, left_sum.astype(F32), precision=lax.Precision.HIGHEST)
    left = inv_act[:, None] * gradient - expand_rows(scaled_act, left_core)
    left = left.astype(BF)
    right_part = jnp.dot(left, scaled_grad, preferred_element_type=F32).astype(BF)
    (right_part, left, keys_z) = phase(right_part, left, keys_z)

    received = [
        here,
        got_here_away,
        got_one,
        got_one_away,
        got_two,
        got_two_away,
        got_three,
        got_three_away,
    ]
    right_sum = deal(right_part.reshape(n_group, rows // n_group, rank), GROUP).astype(BF)
    far = part_grad(coords, received, keys_z, token_scale, (2, 6), 2)
    (far, right_sum, keys_z) = phase(far, right_sum, keys_z)

    ways = (("x", 1), ("x", 3), ("y", 1), ("y", 3))
    via = [shift(f, *way) for f, way in zip(far, ways)]
    right_sum = share(right_sum, GROUP, n_group).reshape(rows, rank)
    near = part_grad(coords, received, keys_z, token_scale, (1, 3, 5, 7), 2)
    (via, near, right_sum, keys_z, left) = phase(via, near, right_sum, keys_z, left)

    free, held = [near[1], near[2], near[5], near[6]], [near[0], near[3], near[4], near[7]]
    got_free = [shift(f, *way) for f, way in zip(free, ways)]
    held = add_terms(held, via)
    right_core = jnp.dot(right_sum.astype(F32), core_grad, precision=lax.Precision.HIGHEST)
    precon = left * inv_grad[None, :] - expand_cols(right_core, scaled_grad)
    total = jnp.full((8, 128), jnp.sum(precon * precon), F32)
    (got_free, held, total, keys_z) = phase(got_free, held, total, keys_z)

    got_held = [shift(h, *way) for h, way in zip(held, ways)]
    total = share(total, GROUP, n_group).sum(0)
    own_a, own_b = part_grad(coords, received, keys_z, token_scale, (0, 4))
    (got_held, own_a, own_b, total) = phase(got_held, own_a, own_b, total)
    sum_a, sum_b = merge(
        [
            [own_a, got_held[0], got_free[0], got_free[1], got_held[1]],
            [own_b, got_held[2], got_free[2], got_free[3], got_held[3]],
        ]
    )
    (sum_a, sum_b, total) = phase(sum_a, sum_b, total)

    got_a = [sum_a[0]] + [shift(sum_a[d], "y", d) for d in (1, 2, 3)]
    got_b = [sum_b[0]] + [shift(sum_b[d], "x", d) for d in (1, 2, 3)]
    total = share(total, DATA, n_data).sum(0)[0, 0]
    root_mean = jnp.sqrt(total / (rows * n_data * cols * n_group) + epsilon)
    update = jnp.minimum(1.0, clip_rms / root_mean) * precon
    factor_grad = finish(got_a, got_b)
    return factor_act, factor_grad, update


def solution(mesh):
    cut = Mesh(mesh.devices.reshape(4, 2, 4, 2, 2), AXES)
    placed = (
        P(AXES, None),
        P(AXES, None),
        P(),
        P(),
        P(),
        P(),
        P(DATA, GROUP),
        P(DATA),
        P(GROUP),
        P(AXES, None),
        P(GROUP + DATA, None),
        P(),
        P(),
    )
    return jax.shard_map(
        local,
        mesh=cut,
        in_specs=placed,
        out_specs=(P(GROUP + DATA, None), P(GROUP + DATA, None), P(DATA, GROUP)),
        check_vma=False,
    )
```

```python
import functools
import jax
import jax.numpy as jnp
import numpy as np
from jax import lax
from jax.experimental import pallas as pl
from jax.experimental.pallas import tpu as pltpu
from jax.sharding import Mesh
from jax.sharding import PartitionSpec as P

BF = jnp.bfloat16
F32 = jnp.float32
HB = 4096
INNER = 256
OUTER = HB // INNER
ROOM = 60 << 20
COST_BYTES = 3_400_000


def cost(us):
    return pl.CostEstimate(flops=us * 550_000_000, bytes_accessed=us * COST_BYTES, transcendentals=0)


def hadamard_table(length):
    table = np.ones((1, 1), np.float32)
    while table.shape[0] < length:
        table = np.block([[table, table], [table, -table]])
    return jnp.asarray(table, BF)


def sketch_kernel(picks, x_ref, sign_ref, table_ref, out_ref, inner, spread, rows):
    block = pl.program_id(0)
    signs = (2 * sign_ref[...] - 1).astype(F32).astype(BF)
    for q in range(OUTER):
        cols = slice(q * INNER, (q + 1) * INNER)
        signed = table_ref[...] * signs[:, cols]
        inner[q] = lax.dot_general(
            signed, x_ref[:, cols], (((1,), (1,)), ((), ())), preferred_element_type=F32
        )

    strip = 8

    def mix(j, carry):
        at = pl.ds(pl.multiple_of(j * strip, strip), strip)
        parts = [inner[q, at, :] for q in range(OUTER)]
        half = 1
        while half < OUTER:
            for low in range(OUTER):
                if low & half == 0:
                    a, b = parts[low], parts[low | half]
                    parts[low], parts[low | half] = a + b, a - b
            half *= 2
        for p in range(OUTER):
            to = pl.multiple_of(block * HB + p * INNER + j * strip, strip)
            spread[pl.ds(to, strip), :] = parts[p]
        return carry

    lax.fori_loop(0, INNER // strip, mix, 0, unroll=2)

    @pl.when(block == pl.num_programs(0) - 1)
    def _():
        count = rows.shape[0]
        group = 16

        def take(i, carry):
            base = pl.multiple_of(i * group, group)
            for k in range(group):
                rows[pl.ds(base + k, 1), :] = spread[pl.ds(picks[base + k], 1), :]
            return carry

        lax.fori_loop(0, count // group, take, 0)
        out_ref[...] = rows[...].T.astype(BF)


def sketch(matrix, signs, picks, table):
    tokens, width = matrix.shape
    count = picks.shape[0]
    return pl.pallas_call(
        sketch_kernel,
        grid_spec=pltpu.PrefetchScalarGridSpec(
            num_scalar_prefetch=1,
            grid=(width // HB,),
            in_specs=[
                pl.BlockSpec((tokens, HB), lambda b, p: (0, b)),
                pl.BlockSpec((1, HB), lambda b, p: (0, b)),
                pl.BlockSpec((INNER, INNER), lambda b, p: (0, 0)),
            ],
            out_specs=pl.BlockSpec((tokens, count), lambda b, p: (0, 0)),
            scratch_shapes=[
                pltpu.VMEM((OUTER, INNER, tokens), F32),
                pltpu.VMEM((width, tokens), F32),
                pltpu.VMEM((count, tokens), F32),
            ],
        ),
        out_shape=jax.ShapeDtypeStruct((tokens, count), BF),
        compiler_params=pltpu.CompilerParams(vmem_limit_bytes=ROOM),
        cost_estimate=cost(2 + width // 2400),
        name="sketch",
    )(picks, matrix, signs[None, :], table)


def turn_kernel(shifts, coords, grad_ref, *refs):
    outs, turned = refs[:-1], refs[-1]
    yhi = pl.program_id(1)
    x, y, core = coords[0], coords[1], coords[3]
    wide = grad_ref.shape[1] // 2
    own = wide // 8
    part = own // 2
    turned[...] = grad_ref[...].T
    for j in range(len(shifts)):

        @pl.when(pl.program_id(0) == j)
        def _(j=j):
            for away in range(2):
                for dx in range(4):
                    for ylo in range(2):
                        dy = (2 * yhi + ylo - y) & 3
                        at = (core ^ away) * wide + ((x + dx) & 3) * (2 * own) + ylo * own
                        at = pl.multiple_of(at, 16)
                        out = outs[2 * j + away]
                        out[dx * 4 + dy] = turned[pl.ds(at, part), :]
                        out[16 + dy * 4 + dx] = turned[pl.ds(at + part, part), :]


def turn(coords, grads, shifts):
    tokens = grads.shape[0]
    wide = grads.shape[1] // 8
    part = wide // 32
    first, last = shifts[0], shifts[-1]

    def slab(i, j, c):
        return (0, ((c[2] + jnp.where(i == 0, first, last)) & 3) * 2 + j)

    count = 2 * len(shifts)
    outs = pl.pallas_call(
        functools.partial(turn_kernel, shifts),
        grid_spec=pltpu.PrefetchScalarGridSpec(
            num_scalar_prefetch=1,
            grid=(len(shifts), 2),
            in_specs=[pl.BlockSpec((tokens, wide), slab)],
            out_specs=[pl.BlockSpec((32, part, tokens), lambda i, j, c: (0, 0, 0))] * count,
            scratch_shapes=[pltpu.VMEM((wide, tokens), BF)],
        ),
        out_shape=[jax.ShapeDtypeStruct((32, part, tokens), BF)] * count,
        compiler_params=pltpu.CompilerParams(vmem_limit_bytes=ROOM),
        cost_estimate=cost(6),
        name="turn",
    )(coords, grads)
    return [o.reshape(-1, tokens) for o in outs]


def turn_act_kernel(act_ref, out_ref, turned):
    z, yhi = pl.program_id(0), pl.program_id(1)
    slim = act_ref.shape[1] // 2
    small = slim // 8
    turned[...] = act_ref[...].T
    for ylo in range(2):
        for side in range(2):
            for xp in range(4):
                at = side * slim + xp * (2 * small) + ylo * small
                out_ref[ylo * 4 + yhi * 2 + side, xp * 4 + z] = turned[at : at + small, :]


def turn_act(acts):
    tokens = acts.shape[0]
    slim = acts.shape[1] // 8
    small = slim // 16
    return pl.pallas_call(
        turn_act_kernel,
        grid=(4, 2),
        in_specs=[pl.BlockSpec((tokens, slim), lambda i, j: (0, i * 2 + j))],
        out_specs=pl.BlockSpec((8, 16, small, tokens), lambda i, j: (0, 0, 0, 0)),
        out_shape=jax.ShapeDtypeStruct((8, 16, small, tokens), BF),
        scratch_shapes=[pltpu.VMEM((slim, tokens), BF)],
        compiler_params=pltpu.CompilerParams(vmem_limit_bytes=ROOM),
        cost_estimate=cost(6),
        name="turn_act",
    )(acts)


def part_kernel(scale, split, coords, *refs):
    rows, given, outs = refs[0:8], refs[8:16], refs[16:]
    total = None
    for d in range(0, 8, 2):
        block = jnp.concatenate([rows[d][...], rows[d + 1][...]], axis=1)
        keys = jnp.concatenate([given[d][...], given[d + 1][...]], axis=0)
        term = jnp.dot(block, keys, preferred_element_type=F32)
        total = term if total is None else total + term
    total = (total * scale).astype(BF)
    if split == 0:
        outs[0][...] = total
        return
    each = total.shape[0] // split
    for j in range(len(outs) // split):

        @pl.when(pl.program_id(0) == j)
        def _(j=j):
            for k in range(split):
                outs[j * split + k][...] = total[k * each : (k + 1) * each]


def part_product(coords, rows, row_specs, keys, key_specs, scale, tile, steps, split):
    tokens, width = rows[0].shape[-1], keys[0].shape[-1]
    if split:
        each, count = tile // split, steps * split
        out_spec = pl.BlockSpec((each, width), lambda i, c: (0, 0))
    else:
        each, count = tile * steps, 1
        out_spec = pl.BlockSpec((tile, width), lambda i, c: (i, 0))
    return pl.pallas_call(
        functools.partial(part_kernel, scale, split),
        grid_spec=pltpu.PrefetchScalarGridSpec(
            num_scalar_prefetch=1,
            grid=(steps,),
            in_specs=row_specs + key_specs,
            out_specs=[out_spec] * count,
        ),
        out_shape=[jax.ShapeDtypeStruct((each, width), BF)] * count,
        compiler_params=pltpu.CompilerParams(vmem_limit_bytes=ROOM),
        cost_estimate=cost(5 + steps * tile // 160),
        name="part_product",
    )(coords, *rows, *keys)


def part_grad(coords, rows, keys, scale, tiles, split=1):
    tile, tokens = rows[0].shape[0] // 8, rows[0].shape[1]
    width = keys.shape[-1]

    def at(i):
        place = tiles[0]
        for j in range(1, len(tiles)):
            place = jnp.where(i >= j, tiles[j], place)
        return place

    def member(d, c):
        return ((c[2] - d // 2) & 3) * 2 + (c[3] ^ (d % 2))

    row_spec = pl.BlockSpec((tile, tokens), lambda i, c: (at(i), 0))
    key_specs = [
        pl.BlockSpec((None, tokens, width), lambda i, c, d=d: (member(d, c), 0, 0))
        for d in range(8)
    ]
    return part_product(
        coords, rows, [row_spec] * 8, [keys] * 8, key_specs, scale, tile, len(tiles), split
    )


def part_act(coords, rows, keys, sibling, scale):
    tile, tokens = rows.shape[1] // 4, rows.shape[2]
    width = sibling.shape[-1]

    def member(d, away, c):
        y = (c[1] - d) & 3
        return (y & 1) * 4 + (y >> 1) * 2 + (c[3] ^ away)

    row_specs = [
        pl.BlockSpec((None, tile, tokens), lambda i, c, d=d, a=a: (member(d, a, c), i, 0))
        for a in range(2)
        for d in range(4)
    ]
    key_specs = [pl.BlockSpec((tokens, width), lambda i, c: (0, 0))] * 4
    key_specs += [pl.BlockSpec((tokens, width), lambda i, c, d=d: (d, 0)) for d in range(4)]
    return part_product(
        coords, [rows] * 8, row_specs, [*keys, *([sibling] * 4)], key_specs, scale, tile, 4, 0
    )[0]


def add_kernel(*refs):
    count = len(refs) // 3
    for j in range(count):
        base, term, out = refs[j], refs[count + j], refs[2 * count + j]
        out[...] = (base[...].astype(F32) + term[...].astype(F32)).astype(BF)


def add_terms(bases, terms):
    rows, width = terms[0].shape
    block = rows // 2
    count = len(bases)
    spec = pl.BlockSpec((block, width), lambda i: (i, 0))
    return pl.pallas_call(
        add_kernel,
        grid=(2,),
        in_specs=[spec] * (2 * count),
        out_specs=[spec] * count,
        out_shape=[jax.ShapeDtypeStruct(b.shape, BF) for b in bases],
        compiler_params=pltpu.CompilerParams(vmem_limit_bytes=ROOM),
        cost_estimate=cost(5),
        name="add_terms",
    )(*bases, *terms)


def merge_kernel(*refs):
    count = len(refs) // 9
    ins, outs = refs[: 5 * count], refs[5 * count :]
    for p in range(count):
        here, *halves = [r[...].astype(F32) for r in ins[5 * p : 5 * p + 5]]
        half = here.shape[0] // 2
        total = [here[:half] + halves[0] + halves[2], here[half:] + halves[1] + halves[3]]
        block = half // 2
        outs[4 * p][...] = total[0][:block]
        outs[4 * p + 1][...] = total[0][block:].astype(BF)
        outs[4 * p + 2][...] = total[1][:block].astype(BF)
        outs[4 * p + 3][...] = total[1][block:].astype(BF)


def merge(groups):
    rows, width = groups[0][0].shape
    block, cols = rows // 4, width // 4
    count = len(groups)
    outs = pl.pallas_call(
        merge_kernel,
        grid=(4,),
        in_specs=(
            [pl.BlockSpec((rows, cols), lambda i: (0, i))]
            + [pl.BlockSpec((rows // 2, cols), lambda i: (0, i))] * 4
        )
        * count,
        out_specs=[pl.BlockSpec((block, cols), lambda i: (0, i))] * (4 * count),
        out_shape=(
            [jax.ShapeDtypeStruct((block, width), F32)]
            + [jax.ShapeDtypeStruct((block, width), BF)] * 3
        )
        * count,
        compiler_params=pltpu.CompilerParams(vmem_limit_bytes=ROOM),
        cost_estimate=cost(7),
        name="merge",
    )(*[a for g in groups for a in g])
    return [outs[4 * p : 4 * p + 4] for p in range(count)]


def finish_kernel(*refs):
    out = refs[-1]
    block = refs[0].shape[0]
    for part in range(2):
        own, *got = refs[4 * part : 4 * part + 4]
        total = own[...]
        for g in got:
            total = total + g[...].astype(F32)
        out[part * block : (part + 1) * block] = total


def finish(first, second):
    rows, width = first[0].shape
    cols = width // 2
    return pl.pallas_call(
        finish_kernel,
        grid=(2,),
        in_specs=[pl.BlockSpec((rows, cols), lambda i: (0, i))] * 8,
        out_specs=pl.BlockSpec((2 * rows, cols), lambda i: (0, i)),
        out_shape=jax.ShapeDtypeStruct((2 * rows, width), F32),
        cost_estimate=cost(4),
        compiler_params=pltpu.CompilerParams(vmem_limit_bytes=ROOM),
        name="finish",
    )(*first, *second)


AXES = ("x", "ylo", "z", "yhi", "core")
GROUP = ("z", "yhi", "core")
DATA = ("x", "ylo")
RING_Y = ("ylo", "yhi")
AROUND_Y = ("ylo", "yhi", "core")
ALONG_Z = ("z", "core")
epsilon = 1e-06
clip_rms = 1.0


def shift(array, axis, step):
    if axis == "y":
        spot = lambda y: (y % 2) * 2 + y // 2
        return lax.ppermute(
            array, RING_Y, [(spot(y), spot((y + step) % 4)) for y in range(4)]
        )
    return lax.ppermute(array, axis, [(i, (i + step) % 4) for i in range(4)])


def swap(array):
    return lax.ppermute(array, "core", [(0, 1), (1, 0)])


def send(array, step, away):
    pairs = [(2 * z + c, 2 * ((z + step) % 4) + (c ^ away)) for z in range(4) for c in range(2)]
    return lax.ppermute(array, ALONG_Z, pairs)


def phase(*values):
    return lax.optimization_barrier(values)


def contract_rows(first_block, second_block):
    return lax.dot_general(
        first_block, second_block, (((0,), (0,)), ((), ())), preferred_element_type=F32
    )


def split_parts(matrix):
    high_part = matrix.astype(BF)
    low_part = (matrix - high_part.astype(F32)).astype(BF)
    return high_part, low_part


def expand_rows(panel, core_product):
    high_part, low_part = split_parts(core_product)
    return jnp.dot(panel, high_part, preferred_element_type=F32) + jnp.dot(
        panel, low_part, preferred_element_type=F32
    )


def expand_cols(core_product, panel):
    high_part, low_part = split_parts(core_product)
    dims = (((1,), (1,)), ((), ()))
    return lax.dot_general(
        high_part, panel, dims, preferred_element_type=F32
    ) + lax.dot_general(low_part, panel, dims, preferred_element_type=F32)


def share(block, axes, n):
    copies = jnp.broadcast_to(block[None], (n,) + block.shape)
    return lax.all_to_all(copies, axes, 0, 0, tiled=True)


def deal(blocks, axes):
    return lax.all_to_all(blocks, axes, 0, 0, tiled=True).astype(F32).sum(0)


def local(
    activations,
    out_grads,
    act_signs,
    grad_signs,
    act_picks,
    grad_picks,
    gradient,
    damped_act,
    damped_grad,
    panel_act,
    panel_grad,
    core_act,
    core_grad,
):
    y = lax.axis_index("yhi") * 2 + lax.axis_index("ylo")
    coords = jnp.stack(
        [lax.axis_index("x"), y, lax.axis_index("z"), lax.axis_index("core")]
    ).astype(jnp.int32)
    token_scale = 1.0 / (activations.shape[0] * lax.axis_size(AXES))
    table = hadamard_table(INNER)
    n_data, n_group = lax.axis_size(DATA), lax.axis_size(GROUP)
    rows, cols = gradient.shape
    rank = panel_act.shape[1]
    inv_act = 1.0 / damped_act
    inv_grad = 1.0 / damped_grad

    here, here_away, two, two_away = turn(coords, out_grads, (0, 2))
    (two, two_away, here_away, coords, panel_act, act_picks, grad_picks, gradient) = phase(
        two, two_away, here_away, coords, panel_act, act_picks, grad_picks, gradient
    )

    got = [send(two, 2, 0), send(two_away, 2, 1), send(here_away, 0, 1)]
    rows_act = share(panel_act, GROUP, n_group).reshape(rows, rank)
    one, one_away, three, three_away = turn(coords, out_grads, (1, 3))
    sketch_act = sketch(activations, act_signs, act_picks, table)
    sketch_grad = sketch(out_grads, grad_signs, grad_picks, table)
    scaled_act = (rows_act * inv_act[:, None]).astype(BF)
    left_part = contract_rows(scaled_act, gradient).astype(BF)
    left_part = left_part.reshape(n_data, rank // n_data, cols)
    panel = jnp.broadcast_to(panel_grad.reshape(1, -1, cols), (n_data, rank // n_data, cols))
    mixed = jnp.concatenate([left_part, panel], axis=1)
    (got, one, one_away, three, three_away, mixed, sketch_grad, sketch_act, scaled_act, activations) = phase(
        got, one, one_away, three, three_away, mixed, sketch_grad, sketch_act, scaled_act, activations
    )
    got_two, got_two_away, got_here_away = got

    keys_z = lax.all_gather(sketch_grad, ALONG_Z, axis=0)
    got = [send(one, 1, 0), send(three, 3, 0), shift(sketch_act, "y", 2)]
    mixed = lax.all_to_all(mixed, DATA, 0, 0, tiled=True)
    for_y = turn_act(activations)
    (got, one_away, three_away, mixed, for_y, sketch_act) = phase(
        got, one_away, three_away, mixed, for_y, sketch_act
    )
    got_one, got_three, keys_two = got
    left_sum = mixed[:, : rank // n_data].astype(F32).sum(0).astype(BF)
    (left_sum, one_away, three_away, sketch_act) = phase(left_sum, one_away, three_away, sketch_act)

    got = [send(one_away, 1, 1), send(three_away, 3, 1)]
    got += [shift(sketch_act, "y", 1), shift(sketch_act, "y", 3)]
    left_sum = share(left_sum, DATA, n_data).reshape(rank, cols)
    rows_grad = mixed[:, rank // n_data :].reshape(cols, rank)
    scaled_grad = (rows_grad * inv_grad[:, None]).astype(BF)
    left_core = jnp.dot(core_act, left_sum.astype(F32), precision=lax.Precision.HIGHEST)
    left = inv_act[:, None] * gradient - expand_rows(scaled_act, left_core)
    left = left.astype(BF)
    right_part = jnp.dot(left, scaled_grad, preferred_element_type=F32).astype(BF)
    (got, left, right_part, keys_z, sketch_act) = phase(got, left, right_part, keys_z, sketch_act)
    got_one_away, got_three_away, keys_one, keys_three = got
    keys_y = [sketch_act, keys_one, keys_two, keys_three]

    rows_y = lax.all_to_all(for_y, AROUND_Y, 0, 0, tiled=True).reshape(8, -1, for_y.shape[-1])
    both = jnp.concatenate(keys_y, axis=0)
    received = [
        here,
        got_here_away,
        got_one,
        got_one_away,
        got_two,
        got_two_away,
        got_three,
        got_three_away,
    ]
    far = part_grad(coords, received, keys_z, token_scale, (2, 6), 2)
    (far, both, keys_z, rows_y) = phase(far, both, keys_z, rows_y)

    ways = (("x", 1), ("x", 3), ("y", 1), ("y", 3))
    via = [shift(f, *way) for f, way in zip(far, ways)]
    right_sum = deal(right_part.reshape(n_group, rows // n_group, rank), GROUP).astype(BF)
    keys_sib = swap(both)
    near = part_grad(coords, received, keys_z, token_scale, (1, 3, 5, 7), 2)
    (via, near, right_sum, keys_z, keys_sib, rows_y) = phase(
        via, near, right_sum, keys_z, keys_sib, rows_y
    )

    free, held = [near[1], near[2], near[5], near[6]], [near[0], near[3], near[4], near[7]]
    got_free = [shift(f, *way) for f, way in zip(free, ways)]
    held = add_terms(held, via)
    right_sum = share(right_sum, GROUP, n_group).reshape(rows, rank)
    partial = part_act(coords, rows_y, keys_y, keys_sib, token_scale)
    (got_free, held, right_sum, partial, left, keys_z) = phase(
        got_free, held, right_sum, partial, left, keys_z
    )
    factor_act = lax.psum_scatter(partial, ("x", "z"), scatter_dimension=0, tiled=True).astype(F32)

    got_held = [shift(h, *way) for h, way in zip(held, ways)]
    right_core = jnp.dot(right_sum.astype(F32), core_grad, precision=lax.Precision.HIGHEST)
    precon = left * inv_grad[None, :] - expand_cols(right_core, scaled_grad)
    total = jnp.full((8, 128), jnp.sum(precon * precon), F32)
    own_a, own_b = part_grad(coords, received, keys_z, token_scale, (0, 4))
    sum_a, sum_b = merge(
        [
            [own_a, got_held[0], got_free[0], got_free[1], got_held[1]],
            [own_b, got_held[2], got_free[2], got_free[3], got_held[3]],
        ]
    )
    total = share(total, GROUP, n_group).sum(0)
    (sum_a, sum_b, total) = phase(sum_a, sum_b, total)

    got_a = [sum_a[0]] + [shift(sum_a[d], "y", d) for d in (1, 2, 3)]
    got_b = [sum_b[0]] + [shift(sum_b[d], "x", d) for d in (1, 2, 3)]
    total = share(total, DATA, n_data).sum(0)[0, 0]
    root_mean = jnp.sqrt(total / (rows * n_data * cols * n_group) + epsilon)
    update = jnp.minimum(1.0, clip_rms / root_mean) * precon
    factor_grad = finish(got_a, got_b)
    return factor_act, factor_grad, update


def solution(mesh):
    cut = Mesh(mesh.devices.reshape(4, 2, 4, 2, 2), AXES)
    placed = (
        P(AXES, None),
        P(AXES, None),
        P(),
        P(),
        P(),
        P(),
        P(DATA, GROUP),
        P(DATA),
        P(GROUP),
        P(AXES, None),
        P(GROUP + DATA, None),
        P(),
        P(),
    )
    return jax.shard_map(
        local,
        mesh=cut,
        in_specs=placed,
        out_specs=(P(GROUP + DATA, None), P(GROUP + DATA, None), P(DATA, GROUP)),
        check_vma=False,
    )
```

```python
import functools
import jax
import jax.numpy as jnp
import numpy as np
from jax import lax
from jax.experimental import pallas as pl
from jax.experimental.pallas import tpu as pltpu
from jax.sharding import Mesh
from jax.sharding import PartitionSpec as P

BF = jnp.bfloat16
F32 = jnp.float32
HB = 4096
INNER = 256
OUTER = HB // INNER
ROOM = 60 << 20
COST_BYTES = 3_400_000


def cost(us):
    return pl.CostEstimate(flops=us * 550_000_000, bytes_accessed=us * COST_BYTES, transcendentals=0)


def hadamard_table(length):
    table = np.ones((1, 1), np.float32)
    while table.shape[0] < length:
        table = np.block([[table, table], [table, -table]])
    return jnp.asarray(table, BF)


def sketch_kernel(picks, x_ref, sign_ref, table_ref, out_ref, inner, spread, rows):
    block = pl.program_id(0)
    signs = (2 * sign_ref[...] - 1).astype(F32).astype(BF)
    for q in range(OUTER):
        cols = slice(q * INNER, (q + 1) * INNER)
        signed = table_ref[...] * signs[:, cols]
        inner[q] = lax.dot_general(
            signed, x_ref[:, cols], (((1,), (1,)), ((), ())), preferred_element_type=F32
        )

    strip = 8

    def mix(j, carry):
        at = pl.ds(pl.multiple_of(j * strip, strip), strip)
        parts = [inner[q, at, :] for q in range(OUTER)]
        half = 1
        while half < OUTER:
            for low in range(OUTER):
                if low & half == 0:
                    a, b = parts[low], parts[low | half]
                    parts[low], parts[low | half] = a + b, a - b
            half *= 2
        for p in range(OUTER):
            to = pl.multiple_of(block * HB + p * INNER + j * strip, strip)
            spread[pl.ds(to, strip), :] = parts[p]
        return carry

    lax.fori_loop(0, INNER // strip, mix, 0, unroll=2)

    @pl.when(block == pl.num_programs(0) - 1)
    def _():
        count = rows.shape[0]
        group = 16

        def take(i, carry):
            base = pl.multiple_of(i * group, group)
            for k in range(group):
                rows[pl.ds(base + k, 1), :] = spread[pl.ds(picks[base + k], 1), :]
            return carry

        lax.fori_loop(0, count // group, take, 0)
        out_ref[...] = rows[...].T.astype(BF)


def sketch(matrix, signs, picks, table):
    tokens, width = matrix.shape
    count = picks.shape[0]
    return pl.pallas_call(
        sketch_kernel,
        grid_spec=pltpu.PrefetchScalarGridSpec(
            num_scalar_prefetch=1,
            grid=(width // HB,),
            in_specs=[
                pl.BlockSpec((tokens, HB), lambda b, p: (0, b)),
                pl.BlockSpec((1, HB), lambda b, p: (0, b)),
                pl.BlockSpec((INNER, INNER), lambda b, p: (0, 0)),
            ],
            out_specs=pl.BlockSpec((tokens, count), lambda b, p: (0, 0)),
            scratch_shapes=[
                pltpu.VMEM((OUTER, INNER, tokens), F32),
                pltpu.VMEM((width, tokens), F32),
                pltpu.VMEM((count, tokens), F32),
            ],
        ),
        out_shape=jax.ShapeDtypeStruct((tokens, count), BF),
        compiler_params=pltpu.CompilerParams(vmem_limit_bytes=ROOM),
        cost_estimate=cost(2 + width // 2400),
        name="sketch",
    )(picks, matrix, signs[None, :], table)


def turn_kernel(shifts, coords, grad_ref, *refs):
    outs, turned = refs[:-1], refs[-1]
    yhi = pl.program_id(1)
    x, y, core = coords[0], coords[1], coords[3]
    wide = grad_ref.shape[1] // 2
    own = wide // 8
    part = own // 2
    turned[...] = grad_ref[...].T
    for j in range(len(shifts)):

        @pl.when(pl.program_id(0) == j)
        def _(j=j):
            for away in range(2):
                for dx in range(4):
                    for ylo in range(2):
                        dy = (2 * yhi + ylo - y) & 3
                        at = (core ^ away) * wide + ((x + dx) & 3) * (2 * own) + ylo * own
                        at = pl.multiple_of(at, 16)
                        out = outs[2 * j + away]
                        out[dx * 4 + dy] = turned[pl.ds(at, part), :]
                        out[16 + dy * 4 + dx] = turned[pl.ds(at + part, part), :]


def turn(coords, grads, shifts):
    tokens = grads.shape[0]
    wide = grads.shape[1] // 8
    part = wide // 32

    def slab(i, j, c):
        step = shifts[0]
        for k in range(1, len(shifts)):
            step = jnp.where(i >= k, shifts[k], step)
        return (0, ((c[2] + step) & 3) * 2 + j)

    count = 2 * len(shifts)
    outs = pl.pallas_call(
        functools.partial(turn_kernel, shifts),
        grid_spec=pltpu.PrefetchScalarGridSpec(
            num_scalar_prefetch=1,
            grid=(len(shifts), 2),
            in_specs=[pl.BlockSpec((tokens, wide), slab)],
            out_specs=[pl.BlockSpec((32, part, tokens), lambda i, j, c: (0, 0, 0))] * count,
            scratch_shapes=[pltpu.VMEM((wide, tokens), BF)],
        ),
        out_shape=[jax.ShapeDtypeStruct((32, part, tokens), BF)] * count,
        compiler_params=pltpu.CompilerParams(vmem_limit_bytes=ROOM),
        cost_estimate=cost(6),
        name="turn",
    )(coords, grads)
    return [o.reshape(-1, tokens) for o in outs]


def turn_act_kernel(act_ref, out_ref, turned):
    z, yhi = pl.program_id(0), pl.program_id(1)
    slim = act_ref.shape[1] // 2
    small = slim // 8
    turned[...] = act_ref[...].T
    for ylo in range(2):
        for side in range(2):
            for xp in range(4):
                at = side * slim + xp * (2 * small) + ylo * small
                out_ref[ylo * 4 + yhi * 2 + side, xp * 4 + z] = turned[at : at + small, :]


def turn_act(acts):
    tokens = acts.shape[0]
    slim = acts.shape[1] // 8
    small = slim // 16
    return pl.pallas_call(
        turn_act_kernel,
        grid=(4, 2),
        in_specs=[pl.BlockSpec((tokens, slim), lambda i, j: (0, i * 2 + j))],
        out_specs=pl.BlockSpec((8, 16, small, tokens), lambda i, j: (0, 0, 0, 0)),
        out_shape=jax.ShapeDtypeStruct((8, 16, small, tokens), BF),
        scratch_shapes=[pltpu.VMEM((slim, tokens), BF)],
        compiler_params=pltpu.CompilerParams(vmem_limit_bytes=ROOM),
        cost_estimate=cost(6),
        name="turn_act",
    )(acts)


def part_kernel(scale, split, coords, *refs):
    rows, given, outs = refs[0:8], refs[8:16], refs[16:]
    total = None
    for d in range(0, 8, 2):
        block = jnp.concatenate([rows[d][...], rows[d + 1][...]], axis=1)
        keys = jnp.concatenate([given[d][...], given[d + 1][...]], axis=0)
        term = jnp.dot(block, keys, preferred_element_type=F32)
        total = term if total is None else total + term
    total = (total * scale).astype(BF)
    if split == 0:
        outs[0][...] = total
        return
    each = total.shape[0] // split
    for j in range(len(outs) // split):

        @pl.when(pl.program_id(0) == j)
        def _(j=j):
            for k in range(split):
                outs[j * split + k][...] = total[k * each : (k + 1) * each]


def part_product(coords, rows, row_specs, keys, key_specs, scale, tile, steps, split):
    tokens, width = rows[0].shape[-1], keys[0].shape[-1]
    if split:
        each, count = tile // split, steps * split
        out_spec = pl.BlockSpec((each, width), lambda i, c: (0, 0))
    else:
        each, count = tile * steps, 1
        out_spec = pl.BlockSpec((tile, width), lambda i, c: (i, 0))
    return pl.pallas_call(
        functools.partial(part_kernel, scale, split),
        grid_spec=pltpu.PrefetchScalarGridSpec(
            num_scalar_prefetch=1,
            grid=(steps,),
            in_specs=row_specs + key_specs,
            out_specs=[out_spec] * count,
        ),
        out_shape=[jax.ShapeDtypeStruct((each, width), BF)] * count,
        compiler_params=pltpu.CompilerParams(vmem_limit_bytes=ROOM),
        cost_estimate=cost(5 + steps * tile // 160),
        name="part_product",
    )(coords, *rows, *keys)


def part_grad(coords, rows, keys, scale, tiles, split=1):
    tile, tokens = rows[0].shape[0] // 8, rows[0].shape[1]
    width = keys.shape[-1]

    def at(i):
        place = tiles[0]
        for j in range(1, len(tiles)):
            place = jnp.where(i >= j, tiles[j], place)
        return place

    def member(d, c):
        return ((c[2] - d // 2) & 3) * 2 + (c[3] ^ (d % 2))

    row_spec = pl.BlockSpec((tile, tokens), lambda i, c: (at(i), 0))
    key_specs = [
        pl.BlockSpec((None, tokens, width), lambda i, c, d=d: (member(d, c), 0, 0))
        for d in range(8)
    ]
    return part_product(
        coords, rows, [row_spec] * 8, [keys] * 8, key_specs, scale, tile, len(tiles), split
    )


def part_act(coords, rows, keys, sibling, scale):
    tile, tokens = rows.shape[1] // 4, rows.shape[2]
    width = sibling.shape[-1]

    def member(d, away, c):
        y = (c[1] - d) & 3
        return (y & 1) * 4 + (y >> 1) * 2 + (c[3] ^ away)

    row_specs = [
        pl.BlockSpec((None, tile, tokens), lambda i, c, d=d, a=a: (member(d, a, c), i, 0))
        for a in range(2)
        for d in range(4)
    ]
    key_specs = [pl.BlockSpec((tokens, width), lambda i, c: (0, 0))] * 4
    key_specs += [pl.BlockSpec((tokens, width), lambda i, c, d=d: (d, 0)) for d in range(4)]
    return part_product(
        coords, [rows] * 8, row_specs, [*keys, *([sibling] * 4)], key_specs, scale, tile, 4, 0
    )[0]


def add_kernel(*refs):
    count = len(refs) // 3
    for j in range(count):
        base, term, out = refs[j], refs[count + j], refs[2 * count + j]
        out[...] = (base[...].astype(F32) + term[...].astype(F32)).astype(BF)


def add_terms(bases, terms):
    rows, width = terms[0].shape
    block = rows // 2
    count = len(bases)
    spec = pl.BlockSpec((block, width), lambda i: (i, 0))
    return pl.pallas_call(
        add_kernel,
        grid=(2,),
        in_specs=[spec] * (2 * count),
        out_specs=[spec] * count,
        out_shape=[jax.ShapeDtypeStruct(b.shape, BF) for b in bases],
        compiler_params=pltpu.CompilerParams(vmem_limit_bytes=ROOM),
        cost_estimate=cost(5),
        name="add_terms",
    )(*bases, *terms)


def merge_kernel(*refs):
    count = len(refs) // 9
    ins, outs = refs[: 5 * count], refs[5 * count :]
    for p in range(count):
        here, *halves = [r[...].astype(F32) for r in ins[5 * p : 5 * p + 5]]
        half = here.shape[0] // 2
        total = [here[:half] + halves[0] + halves[2], here[half:] + halves[1] + halves[3]]
        block = half // 2
        outs[4 * p][...] = total[0][:block]
        outs[4 * p + 1][...] = total[0][block:].astype(BF)
        outs[4 * p + 2][...] = total[1][:block].astype(BF)
        outs[4 * p + 3][...] = total[1][block:].astype(BF)


def merge(groups):
    rows, width = groups[0][0].shape
    block, cols = rows // 4, width // 4
    count = len(groups)
    outs = pl.pallas_call(
        merge_kernel,
        grid=(4,),
        in_specs=(
            [pl.BlockSpec((rows, cols), lambda i: (0, i))]
            + [pl.BlockSpec((rows // 2, cols), lambda i: (0, i))] * 4
        )
        * count,
        out_specs=[pl.BlockSpec((block, cols), lambda i: (0, i))] * (4 * count),
        out_shape=(
            [jax.ShapeDtypeStruct((block, width), F32)]
            + [jax.ShapeDtypeStruct((block, width), BF)] * 3
        )
        * count,
        compiler_params=pltpu.CompilerParams(vmem_limit_bytes=ROOM),
        cost_estimate=cost(7),
        name="merge",
    )(*[a for g in groups for a in g])
    return [outs[4 * p : 4 * p + 4] for p in range(count)]


def finish_kernel(*refs):
    out = refs[-1]
    block = refs[0].shape[0]
    for part in range(2):
        own, *got = refs[4 * part : 4 * part + 4]
        total = own[...]
        for g in got:
            total = total + g[...].astype(F32)
        out[part * block : (part + 1) * block] = total


def finish(first, second):
    rows, width = first[0].shape
    cols = width // 2
    return pl.pallas_call(
        finish_kernel,
        grid=(2,),
        in_specs=[pl.BlockSpec((rows, cols), lambda i: (0, i))] * 8,
        out_specs=pl.BlockSpec((2 * rows, cols), lambda i: (0, i)),
        out_shape=jax.ShapeDtypeStruct((2 * rows, width), F32),
        cost_estimate=cost(4),
        compiler_params=pltpu.CompilerParams(vmem_limit_bytes=ROOM),
        name="finish",
    )(*first, *second)


AXES = ("x", "ylo", "z", "yhi", "core")
GROUP = ("z", "yhi", "core")
DATA = ("x", "ylo")
RING_Y = ("ylo", "yhi")
AROUND_Y = ("ylo", "yhi", "core")
ALONG_Z = ("z", "core")
epsilon = 1e-06
clip_rms = 1.0


def shift(array, axis, step):
    if axis == "y":
        spot = lambda y: (y % 2) * 2 + y // 2
        return lax.ppermute(
            array, RING_Y, [(spot(y), spot((y + step) % 4)) for y in range(4)]
        )
    return lax.ppermute(array, axis, [(i, (i + step) % 4) for i in range(4)])


def swap(array):
    return lax.ppermute(array, "core", [(0, 1), (1, 0)])


def send(array, step, away):
    pairs = [(2 * z + c, 2 * ((z + step) % 4) + (c ^ away)) for z in range(4) for c in range(2)]
    return lax.ppermute(array, ALONG_Z, pairs)


def phase(*values):
    return lax.optimization_barrier(values)


def contract_rows(first_block, second_block):
    return lax.dot_general(
        first_block, second_block, (((0,), (0,)), ((), ())), preferred_element_type=F32
    )


def split_parts(matrix):
    high_part = matrix.astype(BF)
    low_part = (matrix - high_part.astype(F32)).astype(BF)
    return high_part, low_part


def expand_rows(panel, core_product):
    high_part, low_part = split_parts(core_product)
    return jnp.dot(panel, high_part, preferred_element_type=F32) + jnp.dot(
        panel, low_part, preferred_element_type=F32
    )


def expand_cols(core_product, panel):
    high_part, low_part = split_parts(core_product)
    dims = (((1,), (1,)), ((), ()))
    return lax.dot_general(
        high_part, panel, dims, preferred_element_type=F32
    ) + lax.dot_general(low_part, panel, dims, preferred_element_type=F32)


def share(block, axes, n):
    copies = jnp.broadcast_to(block[None], (n,) + block.shape)
    return lax.all_to_all(copies, axes, 0, 0, tiled=True)


def deal(blocks, axes):
    return lax.all_to_all(blocks, axes, 0, 0, tiled=True).astype(F32).sum(0)


def local(
    activations,
    out_grads,
    act_signs,
    grad_signs,
    act_picks,
    grad_picks,
    gradient,
    damped_act,
    damped_grad,
    panel_act,
    panel_grad,
    core_act,
    core_grad,
):
    y = lax.axis_index("yhi") * 2 + lax.axis_index("ylo")
    coords = jnp.stack(
        [lax.axis_index("x"), y, lax.axis_index("z"), lax.axis_index("core")]
    ).astype(jnp.int32)
    token_scale = 1.0 / (activations.shape[0] * lax.axis_size(AXES))
    table = hadamard_table(INNER)
    n_data, n_group = lax.axis_size(DATA), lax.axis_size(GROUP)
    rows, cols = gradient.shape
    rank = panel_act.shape[1]
    inv_act = 1.0 / damped_act
    inv_grad = 1.0 / damped_grad

    two, two_away = turn(coords, out_grads, (2,))
    (two, two_away, coords, panel_act, act_picks, grad_picks, gradient) = phase(
        two, two_away, coords, panel_act, act_picks, grad_picks, gradient
    )

    got = [send(two, 2, 0), send(two_away, 2, 1)]
    rows_act = share(panel_act, GROUP, n_group).reshape(rows, rank)
    here, here_away, one, one_away, three, three_away = turn(coords, out_grads, (0, 1, 3))
    sketch_act = sketch(activations, act_signs, act_picks, table)
    sketch_grad = sketch(out_grads, grad_signs, grad_picks, table)
    scaled_act = (rows_act * inv_act[:, None]).astype(BF)
    left_part = contract_rows(scaled_act, gradient).astype(BF)
    left_part = left_part.reshape(n_data, rank // n_data, cols)
    panel = jnp.broadcast_to(panel_grad.reshape(1, -1, cols), (n_data, rank // n_data, cols))
    mixed = jnp.concatenate([left_part, panel], axis=1)
    (got, here_away, one, one_away, three, three_away, mixed, sketch_grad, sketch_act, scaled_act, activations) = phase(
        got, here_away, one, one_away, three, three_away, mixed, sketch_grad, sketch_act, scaled_act, activations
    )
    got_two, got_two_away = got

    keys_z = lax.all_gather(sketch_grad, ALONG_Z, axis=0)
    got = [send(one, 1, 0), send(three, 3, 0), shift(sketch_act, "y", 2), send(here_away, 0, 1)]
    mixed = lax.all_to_all(mixed, DATA, 0, 0, tiled=True)
    for_y = turn_act(activations)
    (got, one_away, three_away, for_y, sketch_act) = phase(
        got, one_away, three_away, for_y, sketch_act
    )
    got_one, got_three, keys_two, got_here_away = got
    left_sum = mixed[:, : rank // n_data].astype(F32).sum(0).astype(BF)

    got = [send(one_away, 1, 1), send(three_away, 3, 1)]
    got += [shift(sketch_act, "y", 1), shift(sketch_act, "y", 3)]
    left_sum = share(left_sum, DATA, n_data).reshape(rank, cols)
    rows_grad = mixed[:, rank // n_data :].reshape(cols, rank)
    scaled_grad = (rows_grad * inv_grad[:, None]).astype(BF)
    left_core = jnp.dot(core_act, left_sum.astype(F32), precision=lax.Precision.HIGHEST)
    left = inv_act[:, None] * gradient - expand_rows(scaled_act, left_core)
    left = left.astype(BF)
    right_part = jnp.dot(left, scaled_grad, preferred_element_type=F32).astype(BF)
    (got, left, right_part, keys_z, sketch_act) = phase(got, left, right_part, keys_z, sketch_act)
    got_one_away, got_three_away, keys_one, keys_three = got
    keys_y = [sketch_act, keys_one, keys_two, keys_three]

    rows_y = lax.all_to_all(for_y, AROUND_Y, 0, 0, tiled=True).reshape(8, -1, for_y.shape[-1])
    both = jnp.concatenate(keys_y, axis=0)
    received = [
        here,
        got_here_away,
        got_one,
        got_one_away,
        got_two,
        got_two_away,
        got_three,
        got_three_away,
    ]
    far = part_grad(coords, received, keys_z, token_scale, (2, 6), 2)
    (far, both, keys_z, rows_y) = phase(far, both, keys_z, rows_y)

    ways = (("x", 1), ("x", 3), ("y", 1), ("y", 3))
    via = [shift(f, *way) for f, way in zip(far, ways)]
    right_sum = deal(right_part.reshape(n_group, rows // n_group, rank), GROUP).astype(BF)
    keys_sib = swap(both)
    near = part_grad(coords, received, keys_z, token_scale, (1, 3, 5, 7), 2)
    (via, near, right_sum, keys_z, keys_sib, rows_y) = phase(
        via, near, right_sum, keys_z, keys_sib, rows_y
    )

    free, held = [near[1], near[2], near[5], near[6]], [near[0], near[3], near[4], near[7]]
    got_free = [shift(f, *way) for f, way in zip(free, ways)]
    held = add_terms(held, via)
    right_sum = share(right_sum, GROUP, n_group).reshape(rows, rank)
    partial = part_act(coords, rows_y, keys_y, keys_sib, token_scale)
    (got_free, held, right_sum, partial, left, keys_z) = phase(
        got_free, held, right_sum, partial, left, keys_z
    )
    factor_act = lax.psum_scatter(partial, ("x", "z"), scatter_dimension=0, tiled=True).astype(F32)

    got_held = [shift(h, *way) for h, way in zip(held, ways)]
    right_core = jnp.dot(right_sum.astype(F32), core_grad, precision=lax.Precision.HIGHEST)
    precon = left * inv_grad[None, :] - expand_cols(right_core, scaled_grad)
    total = jnp.full((8, 128), jnp.sum(precon * precon), F32)
    own_a, own_b = part_grad(coords, received, keys_z, token_scale, (0, 4))
    sum_a, sum_b = merge(
        [
            [own_a, got_held[0], got_free[0], got_free[1], got_held[1]],
            [own_b, got_held[2], got_free[2], got_free[3], got_held[3]],
        ]
    )
    total = share(total, GROUP, n_group).sum(0)
    (sum_a, sum_b, total) = phase(sum_a, sum_b, total)

    got_a = [sum_a[0]] + [shift(sum_a[d], "y", d) for d in (1, 2, 3)]
    got_b = [sum_b[0]] + [shift(sum_b[d], "x", d) for d in (1, 2, 3)]
    total = share(total, DATA, n_data).sum(0)[0, 0]
    root_mean = jnp.sqrt(total / (rows * n_data * cols * n_group) + epsilon)
    update = jnp.minimum(1.0, clip_rms / root_mean) * precon
    factor_grad = finish(got_a, got_b)
    return factor_act, factor_grad, update


def solution(mesh):
    cut = Mesh(mesh.devices.reshape(4, 2, 4, 2, 2), AXES)
    placed = (
        P(AXES, None),
        P(AXES, None),
        P(),
        P(),
        P(),
        P(),
        P(DATA, GROUP),
        P(DATA),
        P(GROUP),
        P(AXES, None),
        P(GROUP + DATA, None),
        P(),
        P(),
    )
    return jax.shard_map(
        local,
        mesh=cut,
        in_specs=placed,
        out_specs=(P(GROUP + DATA, None), P(GROUP + DATA, None), P(DATA, GROUP)),
        check_vma=False,
    )
```

```python
import functools
import jax
import jax.numpy as jnp
import numpy as np
from jax import lax
from jax.experimental import pallas as pl
from jax.experimental.pallas import tpu as pltpu
from jax.sharding import Mesh
from jax.sharding import PartitionSpec as P

BF = jnp.bfloat16
F32 = jnp.float32
HB = 4096
INNER = 256
OUTER = HB // INNER
ROOM = 60 << 20
COST_BYTES = 3_400_000


def cost(us):
    return pl.CostEstimate(flops=us * 550_000_000, bytes_accessed=us * COST_BYTES, transcendentals=0)


def hadamard_table(length):
    table = np.ones((1, 1), np.float32)
    while table.shape[0] < length:
        table = np.block([[table, table], [table, -table]])
    return jnp.asarray(table, BF)


def sketch_kernel(picks, x_ref, sign_ref, table_ref, out_ref, inner, spread, rows):
    block = pl.program_id(0)
    signs = (2 * sign_ref[...] - 1).astype(F32).astype(BF)
    for q in range(OUTER):
        cols = slice(q * INNER, (q + 1) * INNER)
        signed = table_ref[...] * signs[:, cols]
        inner[q] = lax.dot_general(
            signed, x_ref[:, cols], (((1,), (1,)), ((), ())), preferred_element_type=F32
        )

    strip = 8

    def mix(j, carry):
        at = pl.ds(pl.multiple_of(j * strip, strip), strip)
        parts = [inner[q, at, :] for q in range(OUTER)]
        half = 1
        while half < OUTER:
            for low in range(OUTER):
                if low & half == 0:
                    a, b = parts[low], parts[low | half]
                    parts[low], parts[low | half] = a + b, a - b
            half *= 2
        for p in range(OUTER):
            to = pl.multiple_of(block * HB + p * INNER + j * strip, strip)
            spread[pl.ds(to, strip), :] = parts[p]
        return carry

    lax.fori_loop(0, INNER // strip, mix, 0, unroll=2)

    @pl.when(block == pl.num_programs(0) - 1)
    def _():
        count = rows.shape[0]
        group = 16

        def take(i, carry):
            base = pl.multiple_of(i * group, group)
            for k in range(group):
                rows[pl.ds(base + k, 1), :] = spread[pl.ds(picks[base + k], 1), :]
            return carry

        lax.fori_loop(0, count // group, take, 0)
        out_ref[...] = rows[...].T.astype(BF)


def sketch(matrix, signs, picks, table):
    tokens, width = matrix.shape
    count = picks.shape[0]
    return pl.pallas_call(
        sketch_kernel,
        grid_spec=pltpu.PrefetchScalarGridSpec(
            num_scalar_prefetch=1,
            grid=(width // HB,),
            in_specs=[
                pl.BlockSpec((tokens, HB), lambda b, p: (0, b)),
                pl.BlockSpec((1, HB), lambda b, p: (0, b)),
                pl.BlockSpec((INNER, INNER), lambda b, p: (0, 0)),
            ],
            out_specs=pl.BlockSpec((tokens, count), lambda b, p: (0, 0)),
            scratch_shapes=[
                pltpu.VMEM((OUTER, INNER, tokens), F32),
                pltpu.VMEM((width, tokens), F32),
                pltpu.VMEM((count, tokens), F32),
            ],
        ),
        out_shape=jax.ShapeDtypeStruct((tokens, count), BF),
        compiler_params=pltpu.CompilerParams(vmem_limit_bytes=ROOM),
        cost_estimate=cost(2 + width // 2400),
        name="sketch",
    )(picks, matrix, signs[None, :], table)


def turn_kernel(shifts, coords, grad_ref, *refs):
    outs, turned = refs[:-1], refs[-1]
    yhi = pl.program_id(1)
    x, y, core = coords[0], coords[1], coords[3]
    wide = grad_ref.shape[1] // 2
    own = wide // 8
    part = own // 2
    turned[...] = grad_ref[...].T
    for j in range(len(shifts)):

        @pl.when(pl.program_id(0) == j)
        def _(j=j):
            for away in range(2):
                for dx in range(4):
                    for ylo in range(2):
                        dy = (2 * yhi + ylo - y) & 3
                        at = (core ^ away) * wide + ((x + dx) & 3) * (2 * own) + ylo * own
                        at = pl.multiple_of(at, 16)
                        out = outs[2 * j + away]
                        out[dx * 4 + dy] = turned[pl.ds(at, part), :]
                        out[16 + dy * 4 + dx] = turned[pl.ds(at + part, part), :]


def turn(coords, grads, shifts):
    tokens = grads.shape[0]
    wide = grads.shape[1] // 8
    part = wide // 32

    def slab(i, j, c):
        step = shifts[0]
        for k in range(1, len(shifts)):
            step = jnp.where(i >= k, shifts[k], step)
        return (0, ((c[2] + step) & 3) * 2 + j)

    count = 2 * len(shifts)
    outs = pl.pallas_call(
        functools.partial(turn_kernel, shifts),
        grid_spec=pltpu.PrefetchScalarGridSpec(
            num_scalar_prefetch=1,
            grid=(len(shifts), 2),
            in_specs=[pl.BlockSpec((tokens, wide), slab)],
            out_specs=[pl.BlockSpec((32, part, tokens), lambda i, j, c: (0, 0, 0))] * count,
            scratch_shapes=[pltpu.VMEM((wide, tokens), BF)],
        ),
        out_shape=[jax.ShapeDtypeStruct((32, part, tokens), BF)] * count,
        compiler_params=pltpu.CompilerParams(vmem_limit_bytes=ROOM),
        cost_estimate=cost(6),
        name="turn",
    )(coords, grads)
    return [o.reshape(-1, tokens) for o in outs]


def turn_act_kernel(act_ref, out_ref, turned):
    z, yhi = pl.program_id(0), pl.program_id(1)
    slim = act_ref.shape[1] // 2
    small = slim // 8
    turned[...] = act_ref[...].T
    for ylo in range(2):
        for side in range(2):
            for xp in range(4):
                at = side * slim + xp * (2 * small) + ylo * small
                out_ref[ylo * 4 + yhi * 2 + side, xp * 4 + z] = turned[at : at + small, :]


def turn_act(acts):
    tokens = acts.shape[0]
    slim = acts.shape[1] // 8
    small = slim // 16
    return pl.pallas_call(
        turn_act_kernel,
        grid=(4, 2),
        in_specs=[pl.BlockSpec((tokens, slim), lambda i, j: (0, i * 2 + j))],
        out_specs=pl.BlockSpec((8, 16, small, tokens), lambda i, j: (0, 0, 0, 0)),
        out_shape=jax.ShapeDtypeStruct((8, 16, small, tokens), BF),
        scratch_shapes=[pltpu.VMEM((slim, tokens), BF)],
        compiler_params=pltpu.CompilerParams(vmem_limit_bytes=ROOM),
        cost_estimate=cost(6),
        name="turn_act",
    )(acts)


def part_kernel(scale, split, coords, *refs):
    rows, given, outs = refs[0:8], refs[8:16], refs[16:]
    total = None
    for d in range(0, 8, 2):
        block = jnp.concatenate([rows[d][...], rows[d + 1][...]], axis=1)
        keys = jnp.concatenate([given[d][...], given[d + 1][...]], axis=0)
        term = jnp.dot(block, keys, preferred_element_type=F32)
        total = term if total is None else total + term
    total = (total * scale).astype(BF)
    if split == 0:
        outs[0][...] = total
        return
    each = total.shape[0] // split
    for j in range(len(outs) // split):

        @pl.when(pl.program_id(0) == j)
        def _(j=j):
            for k in range(split):
                outs[j * split + k][...] = total[k * each : (k + 1) * each]


def part_product(coords, rows, row_specs, keys, key_specs, scale, tile, steps, split):
    tokens, width = rows[0].shape[-1], keys[0].shape[-1]
    if split:
        each, count = tile // split, steps * split
        out_spec = pl.BlockSpec((each, width), lambda i, c: (0, 0))
    else:
        each, count = tile * steps, 1
        out_spec = pl.BlockSpec((tile, width), lambda i, c: (i, 0))
    return pl.pallas_call(
        functools.partial(part_kernel, scale, split),
        grid_spec=pltpu.PrefetchScalarGridSpec(
            num_scalar_prefetch=1,
            grid=(steps,),
            in_specs=row_specs + key_specs,
            out_specs=[out_spec] * count,
        ),
        out_shape=[jax.ShapeDtypeStruct((each, width), BF)] * count,
        compiler_params=pltpu.CompilerParams(vmem_limit_bytes=ROOM),
        cost_estimate=cost(5 + steps * tile // 160),
        name="part_product",
    )(coords, *rows, *keys)


def part_grad(coords, rows, keys, scale, tiles, split=1):
    tile, tokens = rows[0].shape[0] // 8, rows[0].shape[1]
    width = keys.shape[-1]

    def at(i):
        place = tiles[0]
        for j in range(1, len(tiles)):
            place = jnp.where(i >= j, tiles[j], place)
        return place

    def member(d, c):
        return ((c[2] - d // 2) & 3) * 2 + (c[3] ^ (d % 2))

    row_spec = pl.BlockSpec((tile, tokens), lambda i, c: (at(i), 0))
    key_specs = [
        pl.BlockSpec((None, tokens, width), lambda i, c, d=d: (member(d, c), 0, 0))
        for d in range(8)
    ]
    return part_product(
        coords, rows, [row_spec] * 8, [keys] * 8, key_specs, scale, tile, len(tiles), split
    )


def part_act(coords, rows, keys, sibling, scale):
    tile, tokens = rows.shape[1] // 4, rows.shape[2]
    width = sibling.shape[-1]

    def member(d, away, c):
        y = (c[1] - d) & 3
        return (y & 1) * 4 + (y >> 1) * 2 + (c[3] ^ away)

    row_specs = [
        pl.BlockSpec((None, tile, tokens), lambda i, c, d=d, a=a: (member(d, a, c), i, 0))
        for a in range(2)
        for d in range(4)
    ]
    key_specs = [pl.BlockSpec((tokens, width), lambda i, c: (0, 0))] * 4
    key_specs += [pl.BlockSpec((tokens, width), lambda i, c, d=d: (d, 0)) for d in range(4)]
    return part_product(
        coords, [rows] * 8, row_specs, [*keys, *([sibling] * 4)], key_specs, scale, tile, 4, 0
    )[0]


def add_kernel(*refs):
    count = len(refs) // 3
    for j in range(count):
        base, term, out = refs[j], refs[count + j], refs[2 * count + j]
        out[...] = (base[...].astype(F32) + term[...].astype(F32)).astype(BF)


def add_terms(bases, terms):
    rows, width = terms[0].shape
    block = rows // 2
    count = len(bases)
    spec = pl.BlockSpec((block, width), lambda i: (i, 0))
    return pl.pallas_call(
        add_kernel,
        grid=(2,),
        in_specs=[spec] * (2 * count),
        out_specs=[spec] * count,
        out_shape=[jax.ShapeDtypeStruct(b.shape, BF) for b in bases],
        compiler_params=pltpu.CompilerParams(vmem_limit_bytes=ROOM),
        cost_estimate=cost(5),
        name="add_terms",
    )(*bases, *terms)


def merge_kernel(*refs):
    count = len(refs) // 9
    ins, outs = refs[: 5 * count], refs[5 * count :]
    for p in range(count):
        here, *halves = [r[...].astype(F32) for r in ins[5 * p : 5 * p + 5]]
        half = here.shape[0] // 2
        total = [here[:half] + halves[0] + halves[2], here[half:] + halves[1] + halves[3]]
        block = half // 2
        outs[4 * p][...] = total[0][:block]
        outs[4 * p + 1][...] = total[0][block:].astype(BF)
        outs[4 * p + 2][...] = total[1][:block].astype(BF)
        outs[4 * p + 3][...] = total[1][block:].astype(BF)


def merge(groups):
    rows, width = groups[0][0].shape
    block, cols = rows // 4, width // 4
    count = len(groups)
    outs = pl.pallas_call(
        merge_kernel,
        grid=(4,),
        in_specs=(
            [pl.BlockSpec((rows, cols), lambda i: (0, i))]
            + [pl.BlockSpec((rows // 2, cols), lambda i: (0, i))] * 4
        )
        * count,
        out_specs=[pl.BlockSpec((block, cols), lambda i: (0, i))] * (4 * count),
        out_shape=(
            [jax.ShapeDtypeStruct((block, width), F32)]
            + [jax.ShapeDtypeStruct((block, width), BF)] * 3
        )
        * count,
        compiler_params=pltpu.CompilerParams(vmem_limit_bytes=ROOM),
        cost_estimate=cost(7),
        name="merge",
    )(*[a for g in groups for a in g])
    return [outs[4 * p : 4 * p + 4] for p in range(count)]


def finish_kernel(*refs):
    out = refs[-1]
    block = refs[0].shape[0]
    for part in range(2):
        own, *got = refs[4 * part : 4 * part + 4]
        total = own[...]
        for g in got:
            total = total + g[...].astype(F32)
        out[part * block : (part + 1) * block] = total


def finish(first, second):
    rows, width = first[0].shape
    cols = width // 2
    return pl.pallas_call(
        finish_kernel,
        grid=(2,),
        in_specs=[pl.BlockSpec((rows, cols), lambda i: (0, i))] * 8,
        out_specs=pl.BlockSpec((2 * rows, cols), lambda i: (0, i)),
        out_shape=jax.ShapeDtypeStruct((2 * rows, width), F32),
        cost_estimate=cost(4),
        compiler_params=pltpu.CompilerParams(vmem_limit_bytes=ROOM),
        name="finish",
    )(*first, *second)


AXES = ("x", "ylo", "z", "yhi", "core")
GROUP = ("z", "yhi", "core")
DATA = ("x", "ylo")
RING_Y = ("ylo", "yhi")
AROUND_Y = ("ylo", "yhi", "core")
ALONG_Z = ("z", "core")
epsilon = 1e-06
clip_rms = 1.0


def shift(array, axis, step):
    if axis == "y":
        spot = lambda y: (y % 2) * 2 + y // 2
        return lax.ppermute(
            array, RING_Y, [(spot(y), spot((y + step) % 4)) for y in range(4)]
        )
    return lax.ppermute(array, axis, [(i, (i + step) % 4) for i in range(4)])


def swap(array):
    return lax.ppermute(array, "core", [(0, 1), (1, 0)])


def send(array, step, away):
    pairs = [(2 * z + c, 2 * ((z + step) % 4) + (c ^ away)) for z in range(4) for c in range(2)]
    return lax.ppermute(array, ALONG_Z, pairs)


def phase(*values):
    return lax.optimization_barrier(values)


def contract_rows(first_block, second_block):
    return lax.dot_general(
        first_block, second_block, (((0,), (0,)), ((), ())), preferred_element_type=F32
    )


def split_parts(matrix):
    high_part = matrix.astype(BF)
    low_part = (matrix - high_part.astype(F32)).astype(BF)
    return high_part, low_part


def expand_rows(panel, core_product):
    high_part, low_part = split_parts(core_product)
    return jnp.dot(panel, high_part, preferred_element_type=F32) + jnp.dot(
        panel, low_part, preferred_element_type=F32
    )


def expand_cols(core_product, panel):
    high_part, low_part = split_parts(core_product)
    dims = (((1,), (1,)), ((), ()))
    return lax.dot_general(
        high_part, panel, dims, preferred_element_type=F32
    ) + lax.dot_general(low_part, panel, dims, preferred_element_type=F32)


def share(block, axes, n):
    copies = jnp.broadcast_to(block[None], (n,) + block.shape)
    return lax.all_to_all(copies, axes, 0, 0, tiled=True)


def deal(blocks, axes):
    return lax.all_to_all(blocks, axes, 0, 0, tiled=True).astype(F32).sum(0)


def local(
    activations,
    out_grads,
    act_signs,
    grad_signs,
    act_picks,
    grad_picks,
    gradient,
    damped_act,
    damped_grad,
    panel_act,
    panel_grad,
    core_act,
    core_grad,
):
    y = lax.axis_index("yhi") * 2 + lax.axis_index("ylo")
    coords = jnp.stack(
        [lax.axis_index("x"), y, lax.axis_index("z"), lax.axis_index("core")]
    ).astype(jnp.int32)
    token_scale = 1.0 / (activations.shape[0] * lax.axis_size(AXES))
    table = hadamard_table(INNER)
    n_data, n_group = lax.axis_size(DATA), lax.axis_size(GROUP)
    rows, cols = gradient.shape
    rank = panel_act.shape[1]
    inv_act = 1.0 / damped_act
    inv_grad = 1.0 / damped_grad

    two, two_away = turn(coords, out_grads, (2,))
    (two, two_away, coords, panel_act, act_picks, grad_picks, gradient) = phase(
        two, two_away, coords, panel_act, act_picks, grad_picks, gradient
    )

    got = [send(two, 2, 0), send(two_away, 2, 1)]
    rows_act = share(panel_act, GROUP, n_group).reshape(rows, rank)
    here, here_away, one, one_away, three, three_away = turn(coords, out_grads, (0, 1, 3))
    sketch_act = sketch(activations, act_signs, act_picks, table)
    sketch_grad = sketch(out_grads, grad_signs, grad_picks, table)
    scaled_act = (rows_act * inv_act[:, None]).astype(BF)
    left_part = contract_rows(scaled_act, gradient).astype(BF)
    left_part = left_part.reshape(n_data, rank // n_data, cols)
    panel = jnp.broadcast_to(panel_grad.reshape(1, -1, cols), (n_data, rank // n_data, cols))
    mixed = jnp.concatenate([left_part, panel], axis=1)
    (got, here_away, one, one_away, three, three_away, mixed, sketch_grad, sketch_act, scaled_act, activations) = phase(
        got, here_away, one, one_away, three, three_away, mixed, sketch_grad, sketch_act, scaled_act, activations
    )
    got_two, got_two_away = got

    keys_z = lax.all_gather(sketch_grad, ALONG_Z, axis=0)
    got = [send(one, 1, 0), send(three, 3, 0), shift(sketch_act, "y", 2), send(here_away, 0, 1)]
    mixed = lax.all_to_all(mixed, DATA, 0, 0, tiled=True)
    for_y = turn_act(activations)
    (got, one_away, three_away, for_y, sketch_act) = phase(
        got, one_away, three_away, for_y, sketch_act
    )
    got_one, got_three, keys_two, got_here_away = got
    left_sum = mixed[:, : rank // n_data].astype(F32).sum(0).astype(BF)

    got = [send(one_away, 1, 1), send(three_away, 3, 1)]
    got += [shift(sketch_act, "y", 1), shift(sketch_act, "y", 3)]
    left_sum = share(left_sum, DATA, n_data).reshape(rank, cols)
    rows_grad = mixed[:, rank // n_data :].reshape(cols, rank)
    scaled_grad = (rows_grad * inv_grad[:, None]).astype(BF)
    left_core = jnp.dot(core_act, left_sum.astype(F32), precision=lax.Precision.HIGHEST)
    left = inv_act[:, None] * gradient - expand_rows(scaled_act, left_core)
    left = left.astype(BF)
    right_part = jnp.dot(left, scaled_grad, preferred_element_type=F32).astype(BF)
    (got, left, right_part, keys_z, sketch_act) = phase(got, left, right_part, keys_z, sketch_act)
    got_one_away, got_three_away, keys_one, keys_three = got
    keys_y = [sketch_act, keys_one, keys_two, keys_three]

    rows_y = lax.all_to_all(for_y, AROUND_Y, 0, 0, tiled=True).reshape(8, -1, for_y.shape[-1])
    both = jnp.concatenate(keys_y, axis=0)
    received = [
        here,
        got_here_away,
        got_one,
        got_one_away,
        got_two,
        got_two_away,
        got_three,
        got_three_away,
    ]
    far = part_grad(coords, received, keys_z, token_scale, (2, 6), 2)
    (far, both, keys_z, rows_y) = phase(far, both, keys_z, rows_y)

    ways = (("x", 1), ("x", 3), ("y", 1), ("y", 3))
    via = [shift(f, *way) for f, way in zip(far, ways)]
    right_sum = deal(right_part.reshape(n_group, rows // n_group, rank), GROUP).astype(BF)
    keys_sib = swap(both)
    near = part_grad(coords, received, keys_z, token_scale, (1, 3, 5, 7), 2)
    (via, near, right_sum, keys_z, keys_sib, rows_y) = phase(
        via, near, right_sum, keys_z, keys_sib, rows_y
    )

    free, held = [near[1], near[2], near[5], near[6]], [near[0], near[3], near[4], near[7]]
    got_free = [shift(f, *way) for f, way in zip(free, ways)]
    held = add_terms(held, via)
    right_sum = share(right_sum, GROUP, n_group).reshape(rows, rank)
    partial = part_act(coords, rows_y, keys_y, keys_sib, token_scale)
    factor_act = lax.psum_scatter(partial, ("x", "z"), scatter_dimension=0, tiled=True).astype(F32)
    (got_free, held, right_sum, partial, left, keys_z) = phase(
        got_free, held, right_sum, partial, left, keys_z
    )

    got_held = [shift(h, *way) for h, way in zip(held, ways)]
    right_core = jnp.dot(right_sum.astype(F32), core_grad, precision=lax.Precision.HIGHEST)
    precon = left * inv_grad[None, :] - expand_cols(right_core, scaled_grad)
    total = jnp.full((8, 128), jnp.sum(precon * precon), F32)
    own_a, own_b = part_grad(coords, received, keys_z, token_scale, (0, 4))
    sum_a, sum_b = merge(
        [
            [own_a, got_held[0], got_free[0], got_free[1], got_held[1]],
            [own_b, got_held[2], got_free[2], got_free[3], got_held[3]],
        ]
    )
    total = share(total, GROUP, n_group).sum(0)
    (sum_a, sum_b, total) = phase(sum_a, sum_b, total)

    got_a = [sum_a[0]] + [shift(sum_a[d], "y", d) for d in (1, 2, 3)]
    got_b = [sum_b[0]] + [shift(sum_b[d], "x", d) for d in (1, 2, 3)]
    total = share(total, DATA, n_data).sum(0)[0, 0]
    root_mean = jnp.sqrt(total / (rows * n_data * cols * n_group) + epsilon)
    update = jnp.minimum(1.0, clip_rms / root_mean) * precon
    factor_grad = finish(got_a, got_b)
    return factor_act, factor_grad, update


def solution(mesh):
    cut = Mesh(mesh.devices.reshape(4, 2, 4, 2, 2), AXES)
    placed = (
        P(AXES, None),
        P(AXES, None),
        P(),
        P(),
        P(),
        P(),
        P(DATA, GROUP),
        P(DATA),
        P(GROUP),
        P(AXES, None),
        P(GROUP + DATA, None),
        P(),
        P(),
    )
    return jax.shard_map(
        local,
        mesh=cut,
        in_specs=placed,
        out_specs=(P(GROUP + DATA, None), P(GROUP + DATA, None), P(DATA, GROUP)),
        check_vma=False,
    )
```
